512 devices in a mesh: tok: 16 (over z), vocab: 16 (over y, x_lo, core), grp: 2 (over x_hi).
Axes of the slice: x: 4 (x_hi: 2, x_lo: 2; x = x_hi * 2 + x_lo), y: 4, z: 16, core: 2. Of those that a mesh axis runs over, the one named last changes fastest.
Arguments:
- logits: bfloat16 [2, 2048, 131072], P('grp', 'tok', 'vocab'), may hold values from -60 to 440
- segment_ids: int32 [2048], P('tok'), may hold values from 0 to 7, as said below
- token_mask: int32 [2048], P('tok'), may hold values from 0 to 1, as said below
- student_head: bfloat16 [32, 16, 256, 1792], P(('vocab', 'grp'), 'tok'), may hold values from -6 to 6
Outputs:
- gradient: bfloat16 [2048, 131072], P('tok', ('vocab', 'grp'))
- hidden_grad: float32 [2048, 1792], P('tok', 'grp')
- distill_loss_total: float32 [], replicated
The draws below stay inside these ranges and needn't reach their ends.
Inputs may be any that keep to these rules, and one draw needn't show every extreme that they name: `segment_ids`: ids never fall along the tokens, and each of the 8 documents holds at least one token. `token_mask`: every document holds at least one token with mask 1.
All inputs are finite; a program needn't handle non-finite values.
Results may differ from the reference program's by a relative error of at most 0.0034.
Values may be sent and summed in bfloat16 or wider, within the bound.
A program may use at most 64 MiB of HBM per device.

```python
import math
import jax
import jax.numpy as jnp
from jax import lax

HS = 1792
SEGS = 8
PACKED_TOKENS = 2048
VOCAB = 131072
W_ROWS = 256
N_TOK = 16
N_VOCAB = 16


def segment_starts(key):
    start_key = jax.random.fold_in(key, 11)
    doc_len = PACKED_TOKENS // SEGS
    offsets = jax.random.randint(start_key, (SEGS,), 0, max(doc_len // 2, 1))
    places = jnp.arange(SEGS, dtype=jnp.int32)
    starts = places * doc_len + offsets
    return jnp.where(places == 0, 0, starts).astype(jnp.int32)


def draw_segment_ids(key, part):
    starts = segment_starts(key)
    position = jnp.arange(PACKED_TOKENS, dtype=jnp.int32)
    above = (position[:, None] >= starts[None, :]).astype(jnp.int32)
    return (jnp.sum(above, axis=1) - 1).astype(jnp.int32)


def draw_token_mask(key, part):
    starts = segment_starts(key)
    key = jax.random.fold_in(key, 2)
    position = jnp.arange(PACKED_TOKENS, dtype=jnp.int32)
    kept = jax.random.randint(key, (PACKED_TOKENS,), 0, 4) > 0
    first = jnp.any(position[:, None] == starts[None, :], axis=1)
    return jnp.logical_or(kept, first).astype(jnp.int32)


def draw_logits(key, part):
    key = jax.random.fold_in(key, 3)
    key_rows, key_cols, key_shared, key_own = jax.random.split(key, 4)
    row_scale = jnp.exp(jax.random.uniform(key_rows, (2, PACKED_TOKENS, 1), jnp.float32, -1.2, 1.1))
    col_scale = jnp.exp(jax.random.uniform(key_cols, (1, 1, VOCAB), jnp.float32, -1.2, 1.1))
    shared_noise = jnp.clip(jax.random.normal(key_shared, (PACKED_TOKENS, VOCAB), jnp.float32), -4.0, 4.0)
    own_noise = jnp.clip(jax.random.normal(key_own, (2, PACKED_TOKENS, VOCAB), jnp.float32), -4.0, 4.0)
    values = (0.8 * shared_noise[None] + 0.6 * own_noise) * row_scale * col_scale
    return values.astype(jnp.bfloat16)


def block_levels(rng, dims, cuts, low, largest):
    def one(dim, blocks):
        steps = jax.random.uniform(jax.random.fold_in(jax.random.fold_in(rng, 6), dim), (blocks,), jnp.float32, low / len(cuts), largest / len(cuts))
        return jnp.repeat(jnp.exp(steps), dims[dim] // blocks).reshape((-1,) + (1,) * (len(dims) - dim - 1))

    factor_of = one(*cuts[0])
    for cut in cuts[1:]:
        factor_of = factor_of * one(*cut)
    return factor_of


def normal_values(rng, shape, spread, reach, shards=(), kind=jnp.bfloat16):
    loudness = block_levels(rng, shape, shards, -0.22, 0.18) if shards else 1.0
    array = jax.random.normal(rng, shape, jnp.float32) * spread * loudness
    return jnp.minimum(jnp.maximum(array, -reach), reach).astype(kind)


def setup_inputs(seed: int = 0) -> dict:
    key_list = jax.random.split(jax.random.key(seed), 5)
    return {
        "logits": draw_logits(jax.random.fold_in(key_list[4], 71), 0),
        "segment_ids": draw_segment_ids(jax.random.fold_in(key_list[4], 71), 0),
        "token_mask": draw_token_mask(jax.random.fold_in(key_list[4], 71), 0),
        "student_head": normal_values(key_list[3], (2 * N_VOCAB, N_TOK, W_ROWS, HS), 1.0, 6.0, ((0, 32), (1, 16))),
    }


SOFTEN_FACTOR = 2.0


def log_total(tempered_logits):
    row_top = jnp.max(tempered_logits, axis=1)
    return row_top + jnp.log(jnp.sum(jnp.exp(tempered_logits - row_top[:, None]), axis=1))


def reference(logits, segment_ids, token_mask, student_head):
    doc_len = PACKED_TOKENS // SEGS
    one_hot = (segment_ids[:, None] == jnp.arange(SEGS, dtype=jnp.int32)[None, :]).astype(jnp.float32)
    masked = token_mask.astype(jnp.float32)
    counts = jnp.sum(one_hot * masked[:, None], axis=0)
    own_size = jnp.sum(one_hot * counts[None, :], axis=1)
    token_factor = masked * doc_len / own_size
    head_matrix = student_head.reshape(VOCAB, HS)
    block = math.gcd(PACKED_TOKENS, 128)
    block_count = PACKED_TOKENS // block
    teacher_blocks = logits[0].reshape(block_count, block, -1)
    student_blocks = logits[1].reshape(block_count, block, -1)
    weight_blocks = token_factor.reshape(block_count, block)

    def one_block(pieces):
        teacher_slice, student_slice, weight_slice = pieces
        teacher_tempered = teacher_slice.astype(jnp.float32) / SOFTEN_FACTOR
        student_tempered = student_slice.astype(jnp.float32) / SOFTEN_FACTOR
        log_teacher = teacher_tempered - log_total(teacher_tempered)[:, None]
        log_student = student_tempered - log_total(student_tempered)[:, None]
        teacher_probs = jnp.exp(log_teacher)
        student_probs = jnp.exp(log_student)
        kl_rows = jnp.sum(teacher_probs * (log_teacher - log_student), axis=1)
        gradient_slice = (SOFTEN_FACTOR * weight_slice[:, None] * (student_probs - teacher_probs)).astype(jnp.bfloat16)
        hidden_part = jnp.dot(gradient_slice, head_matrix, preferred_element_type=jnp.float32)
        return gradient_slice, hidden_part, kl_rows

    grads, hiddens, divergence_blocks = lax.map(one_block, (teacher_blocks, student_blocks, weight_blocks))
    gradient = grads.reshape(PACKED_TOKENS, -1)
    hidden_grad = hiddens.reshape(PACKED_TOKENS, HS)
    distill_loss_total = SOFTEN_FACTOR * SOFTEN_FACTOR * jnp.sum(token_factor * divergence_blocks.reshape(-1)) / PACKED_TOKENS
    return gradient, hidden_grad, distill_loss_total
```

```python
import functools

import jax
import jax.numpy as jnp
from jax import lax
from jax.experimental import pallas as pl
from jax.experimental.pallas import tpu as pltpu
from jax.sharding import PartitionSpec as P

SEGS = 8
SOFTEN = 2.0
NT = 16
ROWS = 128
HALF = 64
TH = 32
BLK = 256
COLS = 4096
HS = 1792
HH = 896
OFF = (0, 1, 7, 2, 6, 3, 5, 4)
MESH = pl.DeviceIdType.MESH
F32 = jnp.float32
BF16 = jnp.bfloat16


def kernel(
    lg_hbm, seg_ref, mask_ref, head_hbm,
    grad_out, hid_out, loss_out,
    lg, a_buf, gbuf, gnat, grx, hb, pb, rb, rsum, zs, zr, fb,
    sc, col, st, stc, sb, cz, cm, lz, lm, lp, lc,
    s_loc, x_s, x_r, h_s, h_r, c_s, c_r, t_s, t_r, g_s, g_r, o_s, o_r,
    p_s, p_r, z_s, z_r, f_s, f_r, l_s, l_r,
):
    z = lax.axis_index("tok")
    v = lax.axis_index("vocab")
    g = lax.axis_index("grp")
    c = v % 2
    xl = (v // 2) % 2
    y = v // 4
    j = v // 2
    par = z % 2
    oc = 1 - c
    og = 1 - g
    ov = v + 1 - 2 * c
    mate = (z + 1 + 14 * ((z + c) % 2)) % NT
    my_pos = (z + c) % 2

    def plane(r):
        h, a, b = r // 8, (r // 2) % 4, r % 2
        y2 = (y + 4 - a) % 4
        x2 = (xl + 2 - b) % 2
        g2 = (g + 2 - h) % 2
        return y2 * 2 + x2, g2, (z, y2 * 4 + x2 * 2 + c, g2)

    def column(p):
        return (z + NT - 2 * OFF[p]) % NT

    def send(src, dst, ss, rs, dev):
        copy = pltpu.make_async_remote_copy(
            src_ref=src, dst_ref=dst, send_sem=ss, recv_sem=rs, device_id=dev, device_id_type=MESH
        )
        copy.start()

    def wait(ref, sem):
        pltpu.make_async_copy(ref, ref, sem).wait()

    core_mate = (z, ov, g)

    in_logits = pltpu.make_async_copy(lg_hbm, lg, s_loc.at[0])
    in_logits.start()
    in_head = pltpu.make_async_copy(head_hbm, hb.at[c, my_pos], s_loc.at[1])
    in_head.start()
    mine = pl.ds(pl.multiple_of(HALF * c, HALF), HALF)
    own_cols = pl.ds(pl.multiple_of(COLS * g, COLS), COLS)
    in_own = pltpu.make_async_copy(lg_hbm.at[mine, own_cols], a_buf.at[g, c], s_loc.at[2])
    in_own.start()

    barrier = pltpu.get_barrier_semaphore()
    for dev in [core_mate, (z, ov, og), (mate, v, g)]:
        pl.semaphore_signal(barrier, inc=1, device_id=dev, device_id_type=MESH)
    for r in range(1, 16):
        pl.semaphore_signal(barrier, inc=1, device_id=plane(r)[2], device_id_type=MESH)
    for p in range(1, 8):
        pl.semaphore_signal(barrier, inc=1, device_id=(column(p), v, g), device_id_type=MESH)
    pl.semaphore_wait(barrier, 25)

    other_cols = pl.ds(pl.multiple_of(COLS * og, COLS), COLS)
    for th in range(2):
        dst = a_buf.at[g, c, pl.ds(TH * th, TH)]
        rows_same = pl.ds(pl.multiple_of(HALF * c + TH * th, TH), TH)
        rows_other = pl.ds(pl.multiple_of(HALF * oc + TH * th, TH), TH)
        send(lg_hbm.at[rows_same, other_cols], dst, x_s.at[th, 1], x_r.at[th, 1], (z, v, og))
        send(lg_hbm.at[rows_other, other_cols], dst, x_s.at[th, 2], x_r.at[th, 2], (z, ov, og))
        send(lg_hbm.at[rows_other, own_cols], dst, x_s.at[th, 0], x_r.at[th, 0], core_mate)

    docs = lax.broadcasted_iota(jnp.int32, (SEGS, ROWS), 0)
    member = (seg_ref[...] == docs).astype(F32)
    masked = mask_ref[...].astype(F32)
    cz[0] = member * masked
    for p in range(1, 8):
        send(cz.at[0], cz.at[p], c_s.at[0], c_r.at[0], (column(p), v, g))

    in_head.wait()
    send(hb.at[c, my_pos], hb.at[c, my_pos], h_s.at[0], h_r.at[0], (mate, v, g))
    send(hb.at[c, my_pos], hb.at[c, my_pos], h_s.at[1], h_r.at[1], core_mate)

    in_logits.wait()
    lane = lax.broadcasted_iota(jnp.int32, (16, 128), 1)

    def stat_rows(i, carry):
        rows = pl.ds(pl.multiple_of(i * 16, 16), 16)
        top = jnp.max(lg[rows, :].astype(F32), axis=1, keepdims=True) * (1.0 / SOFTEN)
        mass = jnp.sum(
            jnp.exp(lg[rows, :].astype(F32) * (1.0 / SOFTEN) - top), axis=1, keepdims=True
        )
        sc[rows, :] = jnp.where(lane == 0, top, mass)
        return carry

    lax.fori_loop(0, ROWS // 16, stat_rows, 0)
    st[0] = sc[...].T[:8]
    send(st.at[0], st.at[1], t_s.at[0], t_r.at[0], core_mate)

    wait(cz.at[pl.ds(1, 7)], c_r.at[0])
    part = cz[0]
    for p in range(1, 8):
        part = part + cz[p]
    cm[0] = part
    send(cm.at[0], cm.at[1], c_s.at[1], c_r.at[1], (mate, v, g))

    wait(st.at[1], t_r.at[0])
    top = jnp.maximum(st[0, 0:1, :], st[1, 0:1, :])
    mass = st[0, 1:2, :] * jnp.exp(st[0, 0:1, :] - top) + st[1, 1:2, :] * jnp.exp(st[1, 0:1, :] - top)
    sub = lax.broadcasted_iota(jnp.int32, (8, ROWS), 0)
    sb[0] = jnp.where(sub == 0, top, mass)
    for r in range(1, 16):
        send(sb.at[0], sb.at[r], t_s.at[1], t_r.at[1], plane(r)[2])

    wait(cm.at[1], c_r.at[1])
    sizes = jnp.sum(cm[0] + cm[1], axis=1, keepdims=True)
    own_size = jnp.sum(member * sizes, axis=0, keepdims=True)
    weight = masked * (NT * ROWS // SEGS) / own_size

    wait(sb.at[pl.ds(1, 15)], t_r.at[1])

    def lse(first):
        top = sb[first, 0:1, :]
        for r in range(first + 1, first + 8):
            top = jnp.maximum(top, sb[r, 0:1, :])
        mass = jnp.zeros_like(top)
        for r in range(first, first + 8):
            mass = mass + sb[r, 1:2, :] * jnp.exp(sb[r, 0:1, :] - top)
        return top + jnp.log(mass)

    own_lse, other_lse = lse(0), lse(8)
    teacher_lse = jnp.where(g == 0, own_lse, other_lse)
    student_lse = jnp.where(g == 0, other_lse, own_lse)
    sc[...] = jnp.zeros_like(sc)
    sc[0:8, :] = jnp.where(sub == 0, teacher_lse, jnp.where(sub == 1, student_lse, weight))
    col[...] = sc[...].T

    loss_acc = jnp.zeros((TH, 128), F32)
    for th in range(2):
        if th == 0:
            in_own.wait()
        wait(a_buf.at[g, oc, pl.ds(TH * th, TH)], x_r.at[th, 0])
        wait(a_buf.at[og, c, pl.ds(TH * th, TH)], x_r.at[th, 1])
        wait(a_buf.at[og, oc, pl.ds(TH * th, TH)], x_r.at[th, 2])
        rows = pl.ds(TH * th, TH)
        stats = col[pl.ds(pl.multiple_of(HALF * c + TH * th, TH), TH), :]
        t_lse, s_lse, wgt = stats[:, 0:1], stats[:, 1:2], stats[:, 2:3]
        scale = SOFTEN * wgt
        for p in list(range(1, 8)) + [0]:
            i = (z // 2 + 8 - OFF[p]) % 8
            blocks = (
                (0, 2 * i),
                (0, 2 * i + 1),
                (1, (2 * i + 15 + 2 * par) % 16),
                (1, (2 * i + 2 * par) % 16),
            )
            for kb, (b, k) in enumerate(blocks):
                cols = pl.ds(pl.multiple_of(BLK * k, BLK), BLK)
                log_t = a_buf[0, b, rows, cols].astype(F32) * (1.0 / SOFTEN) - t_lse
                log_s = a_buf[1, b, rows, cols].astype(F32) * (1.0 / SOFTEN) - s_lse
                prob_t = jnp.exp(log_t)
                prob_s = jnp.exp(log_s)
                grad = (scale * (prob_s - prob_t)).astype(BF16)
                term = prob_t * (log_t - log_s)
                loss_acc = loss_acc + wgt * (term[:, :128] + term[:, 128:])
                gnat[b, rows, cols] = grad
                if p == 0:
                    grx[th, 0, :, kb * BLK:(kb + 1) * BLK] = grad
                else:
                    gbuf[th, p, :, kb * BLK:(kb + 1) * BLK] = grad
            if p:
                send(gbuf.at[th, p], grx.at[th, p], g_s.at[th], g_r.at[th, p // 4], (column(p), v, g))

    out_own = pltpu.make_async_copy(gnat.at[c], grad_out.at[mine, :], s_loc.at[3])
    out_own.start()
    send(gnat.at[oc], grad_out.at[mine, :], o_s, o_r, core_mate)

    lz[0] = loss_acc[0:8] + loss_acc[8:16] + loss_acc[16:24] + loss_acc[24:32]
    for p in range(1, 8):
        send(lz.at[0], lz.at[p], l_s.at[0], l_r.at[0], (column(p), v, g))

    wait(hb.at[c, 1 - my_pos], h_r.at[0])
    send(hb.at[c, 1 - my_pos], hb.at[c, 1 - my_pos], h_s.at[2], h_r.at[2], core_mate)
    wait(hb.at[oc, (z + oc) % 2], h_r.at[1])
    wait(hb.at[oc, 1 - (z + oc) % 2], h_r.at[2])

    out_row = lax.broadcasted_iota(jnp.int32, (128, 128), 0)
    in_row = lax.broadcasted_iota(jnp.int32, (128, 128), 1)
    source = ((out_row // 4) % 4) * TH + (out_row // 16) * 4 + out_row % 4
    order = (in_row == source).astype(F32).astype(BF16)

    def multiply(q):
        th, bh = q // 2, q % 2
        if bh == 0:
            wait(grx.at[th, pl.ds(1, 3)], g_r.at[th, 0])
        else:
            wait(grx.at[th, pl.ds(4, 4)], g_r.at[th, 1])
        x = grx[th, 4 * bh:4 * bh + 4].reshape(128, 4 * BLK)
        x = jnp.dot(order, x, preferred_element_type=F32).astype(BF16)
        for gg in range(2):
            part = jnp.dot(
                x[:, :512], hb[0, :, :, HH * gg:HH * gg + HH].reshape(512, HH), preferred_element_type=F32
            ) + jnp.dot(
                x[:, 512:], hb[1, :, :, HH * gg:HH * gg + HH].reshape(512, HH), preferred_element_type=F32
            )
            pb[q, gg] = part.astype(BF16).reshape(8, 16, HH)
        for r in range(1, 16):
            j2, g2, dev = plane(r)
            send(pb.at[q, g2, j2], rb.at[q, r], p_s.at[q], p_r.at[q], dev)

    def reduce(q):
        wait(rb.at[q, pl.ds(1, 15)], p_r.at[q])
        total = pb[q, g, j].astype(F32)
        for r in range(1, 16):
            total = total + rb[q, r].astype(F32)
        rsum[q] = total

    def spread(bh):
        for bb in range(4):
            p = 4 * bh + bb
            zs[p] = jnp.concatenate([rsum[bh, 4 * bb:4 * bb + 4], rsum[2 + bh, 4 * bb:4 * bb + 4]], axis=0)
            if p:
                dev = ((z + 2 * OFF[p]) % NT, v, g)
                send(zs.at[p], zr.at[p], z_s.at[bh], z_r.at[bh], dev)

    multiply(0)
    wait(lz.at[pl.ds(1, 7)], l_r.at[0])
    part = lz[0]
    for p in range(1, 8):
        part = part + lz[p]
    lm[0] = part
    send(lm.at[0], lm.at[1], l_s.at[1], l_r.at[1], (mate, v, g))
    multiply(1)
    reduce(0)
    wait(lm.at[1], l_r.at[1])
    lp[0] = lm[0] + lm[1]
    for r in range(1, 16):
        send(lp.at[0], lp.at[r], l_s.at[2], l_r.at[2], plane(r)[2])
    multiply(2)
    reduce(1)
    wait(lp.at[pl.ds(1, 15)], l_r.at[2])
    part = lp[0]
    for r in range(1, 16):
        part = part + lp[r]
    lc[0] = part
    send(lc.at[0], lc.at[1], l_s.at[3], l_r.at[3], core_mate)
    multiply(3)
    reduce(2)
    spread(0)
    wait(lc.at[1], l_r.at[3])
    loss_out[...] = (
        jnp.sum(lc[0] + lc[1], keepdims=True) * (SOFTEN * SOFTEN) / (NT * ROWS)
    )
    reduce(3)
    spread(1)

    wait(zr.at[pl.ds(1, 3)], z_r.at[0])
    wait(zr.at[pl.ds(4, 4)], z_r.at[1])
    total = zs[0]
    for p in range(1, 8):
        total = total + zr[p]
    fb[j] = total
    for r in range(1, 8):
        send(fb.at[j], fb.at[j], f_s.at[0], f_r.at[0], plane(r)[2])
    wait(fb.at[pl.ds(0, 7)], f_r.at[0])
    for th in range(2):
        for jj in range(4):
            rows = pl.ds(pl.multiple_of(HALF * c + TH * th + 8 * jj, 8), 8)
            hid_out[rows, :] = jnp.concatenate(
                [fb[2 * jj, 4 * th:4 * th + 4], fb[2 * jj + 1, 4 * th:4 * th + 4]], axis=0
            )
    send(hid_out.at[mine, :], hid_out.at[mine, :], f_s.at[1], f_r.at[1], core_mate)

    for th in range(2):
        for k in range(3):
            wait(a_buf.at[0, 0, pl.ds(0, TH)], x_s.at[th, k])
        wait(grx.at[th, pl.ds(1, 7)], g_s.at[th])
    for k in range(3):
        wait(hb.at[0, 0], h_s.at[k])
    wait(cz.at[pl.ds(1, 7)], c_s.at[0])
    wait(cm.at[1], c_s.at[1])
    wait(st.at[1], t_s.at[0])
    wait(sb.at[pl.ds(1, 15)], t_s.at[1])
    out_own.wait()
    wait(gnat.at[0], o_s)
    wait(grad_out.at[pl.ds(pl.multiple_of(HALF * oc, HALF), HALF), :], o_r)
    for q in range(4):
        wait(rb.at[q, pl.ds(1, 15)], p_s.at[q])
    wait(zr.at[pl.ds(1, 3)], z_s.at[0])
    wait(zr.at[pl.ds(4, 4)], z_s.at[1])
    wait(fb.at[pl.ds(0, 7)], f_s.at[0])
    wait(lz.at[pl.ds(1, 7)], l_s.at[0])
    wait(lm.at[1], l_s.at[1])
    wait(lp.at[pl.ds(1, 15)], l_s.at[2])
    wait(lc.at[1], l_s.at[3])
    wait(hid_out.at[mine, :], f_s.at[1])
    wait(hid_out.at[pl.ds(pl.multiple_of(HALF * oc, HALF), HALF), :], f_r.at[1])


def per_device(logits, segment_ids, token_mask, student_head):
    dma = pltpu.SemaphoreType.DMA
    any_space = pl.BlockSpec(memory_space=pl.ANY)
    vmem_space = pl.BlockSpec(memory_space=pltpu.VMEM)
    grad, hidden, loss = pl.pallas_call(
        kernel,
        out_shape=(
            jax.ShapeDtypeStruct((ROWS, COLS), BF16),
            jax.ShapeDtypeStruct((ROWS, HH), F32),
            jax.ShapeDtypeStruct((1, 1), F32),
        ),
        in_specs=[any_space, vmem_space, vmem_space, any_space],
        out_specs=(any_space, vmem_space, vmem_space),
        scratch_shapes=[
            pltpu.VMEM((ROWS, 2 * COLS), BF16),
            pltpu.VMEM((2, 2, HALF, COLS), BF16),
            pltpu.VMEM((2, 8, TH, 4 * BLK), BF16),
            pltpu.VMEM((2, HALF, COLS), BF16),
            pltpu.VMEM((2, 8, TH, 4 * BLK), BF16),
            pltpu.VMEM((2, 2, BLK, HS), BF16),
            pltpu.VMEM((4, 2, 8, 16, HH), BF16),
            pltpu.VMEM((4, 16, 16, HH), BF16),
            pltpu.VMEM((4, 16, HH), F32),
            pltpu.VMEM((8, 8, HH), F32),
            pltpu.VMEM((8, 8, HH), F32),
            pltpu.VMEM((8, 8, HH), F32),
            pltpu.VMEM((128, 128), F32),
            pltpu.VMEM((128, 128), F32),
            pltpu.VMEM((2, 8, 128), F32),
            pltpu.VMEM((2, 8, 128), F32),
            pltpu.VMEM((16, 8, 128), F32),
            pltpu.VMEM((8, 8, 128), F32),
            pltpu.VMEM((2, 8, 128), F32),
            pltpu.VMEM((8, 8, 128), F32),
            pltpu.VMEM((2, 8, 128), F32),
            pltpu.VMEM((16, 8, 128), F32),
            pltpu.VMEM((2, 8, 128), F32),
            dma((4,)),
            dma((2, 3)), dma((2, 3)),
            dma((3,)), dma((3,)),
            dma((2,)), dma((2,)),
            dma((2,)), dma((2,)),
            dma((2,)), dma((2, 2)),
            dma, dma,
            dma((4,)), dma((4,)),
            dma((2,)), dma((2,)),
            dma((2,)), dma((2,)),
            dma((4,)), dma((4,)),
        ],
        compiler_params=pltpu.CompilerParams(
            collective_id=0, has_side_effects=True, vmem_limit_bytes=40 * 1024 * 1024
        ),
        cost_estimate=pl.CostEstimate(
            flops=2 * ROWS * COLS * HS, bytes_accessed=6 * 1024 * 1024, transcendentals=3 * ROWS * COLS
        ),
        name="distill",
    )(
        logits.reshape(ROWS, 2 * COLS),
        segment_ids.reshape(1, ROWS),
        token_mask.reshape(1, ROWS),
        student_head.reshape(BLK, HS),
    )
    return grad, hidden, loss.reshape(())


def solution(mesh):
    placed = (P("grp", "tok", "vocab"), P("tok"), P("tok"), P(("vocab", "grp"), "tok", None, None))
    return jax.shard_map(
        per_device,
        mesh=mesh,
        in_specs=placed,
        out_specs=(P("tok", ("vocab", "grp")), P("tok", "grp"), P()),
        check_vma=False,
    )
```

```python
import jax
import jax.numpy as jnp
from jax import lax
from jax.experimental import pallas as pl
from jax.experimental.pallas import tpu as pltpu
from jax.sharding import PartitionSpec as P

SEGS = 8
SOFTEN = 2.0
NT = 16
ROWS = 128
HALF = 64
TH = 32
BLK = 256
COLS = 4096
HS = 1792
HH = 896
VMEM_BYTES = 54 * 1024 * 1024
MESH = pl.DeviceIdType.MESH
F32 = jnp.float32
BF16 = jnp.bfloat16
LAST = 7


def off(p):
    return (4 + ((p + 1) // 2) * (1 - 2 * (p % 2))) % 8


def kernel(
    lg_hbm, seg_hbm, mask_hbm, head_hbm,
    grad_out, hid_out, loss_out,
    lg, ao, gb, gn, grx, hb, pb, rb, rsum, zs, zr, own, fb,
    sc, col, st, sb, cz, cm, acc, lz, lm, lp, lc, seg_ref, mask_ref,
    s_loc, x_s, x_r, h_s, h_r, c_s, c_r, t_s, t_r, g_s, g_r,
    p_s, p_r, z_s, z_r, f_s, f_r, l_s, l_r,
):
    z = lax.axis_index("tok")
    v = lax.axis_index("vocab")
    g = lax.axis_index("grp")
    c = v % 2
    xl = (v // 2) % 2
    y = v // 4
    j = v // 2
    par = z % 2
    oc = 1 - c
    og = 1 - g
    ov = v + 1 - 2 * c
    mate = (z + 1 + 14 * ((z + c) % 2)) % NT
    my_pos = (z + c) % 2

    def plane(r):
        h, a, b = r // 8, (r // 2) % 4, r % 2
        y2 = (y + 4 - a) % 4
        x2 = (xl + 2 - b) % 2
        g2 = (g + 2 - h) % 2
        return y2 * 2 + x2, g2

    def plane_dev(r, core):
        j2, g2 = plane(r)
        return (z, j2 * 2 + core, g2)

    def column(p):
        return (z + NT - 2 * off(p)) % NT

    def send(src, dst, ss, rs, dev):
        copy = pltpu.make_async_remote_copy(
            src_ref=src, dst_ref=dst, send_sem=ss, recv_sem=rs, device_id=dev, device_id_type=MESH
        )
        copy.start()

    def wait(ref, sem):
        pltpu.make_async_copy(ref, ref, sem).wait()

    def loop(first, last, body):
        def step(i, carry):
            body(i)
            return carry

        lax.fori_loop(first, last, step, 0)

    core_mate = (z, ov, g)

    in_logits = pltpu.make_async_copy(lg_hbm, lg, s_loc.at[0])
    in_logits.start()
    in_head = pltpu.make_async_copy(head_hbm, hb.at[c, my_pos], s_loc.at[1])
    in_head.start()
    in_seg = pltpu.make_async_copy(seg_hbm, seg_ref, s_loc.at[2])
    in_seg.start()
    in_mask = pltpu.make_async_copy(mask_hbm, mask_ref, s_loc.at[3])
    in_mask.start()

    barrier = pltpu.get_barrier_semaphore()

    def greet(dev):
        pl.semaphore_signal(barrier, inc=1, device_id=dev, device_id_type=MESH)

    greet((mate, v, g))
    loop(1, 16, lambda r: greet(plane_dev(r, c)))
    loop(0, 8, lambda r: greet(plane_dev(r, oc)))

    def greet_column(p):
        greet((column(p), v, g))
        greet((column(p), ov, g))

    loop(0, LAST, greet_column)

    in_logits.wait()
    lane = lax.broadcasted_iota(jnp.int32, (16, 128), 1)

    def stat_rows(i):
        rows = pl.ds(pl.multiple_of(i * 16, 16), 16)
        top = jnp.max(lg[rows, :].astype(F32), axis=1, keepdims=True) * (1.0 / SOFTEN)
        mass = jnp.sum(
            jnp.exp(lg[rows, :].astype(F32) * (1.0 / SOFTEN) - top), axis=1, keepdims=True
        )
        sc[rows, :] = jnp.where(lane == 0, top, mass)

    loop(0, ROWS // 16, stat_rows)
    st[0] = sc[...].T[:8]
    pl.semaphore_wait(barrier, 38)

    other_cols = pl.ds(pl.multiple_of(COLS * og, COLS), COLS)

    def exchange(t):
        rows = pl.ds(TH * t, TH)
        send(lg_hbm.at[rows, other_cols], ao.at[rows], x_s.at[t], x_r.at[t], (z, v, og))

    send(st.at[0], st.at[1], t_s.at[0], t_r.at[0], core_mate)
    exchange(0)
    exchange(1)

    in_seg.wait()
    in_mask.wait()
    docs = lax.broadcasted_iota(jnp.int32, (SEGS, ROWS), 0)
    member = (seg_ref[...] == docs).astype(F32)
    masked = mask_ref[...].astype(F32)
    cz[LAST] = member * masked
    loop(0, LAST, lambda p: send(cz.at[LAST], cz.at[p], c_s.at[0], c_r.at[0], (column(p), v, g)))

    in_head.wait()
    send(hb.at[c, my_pos], hb.at[c, my_pos], h_s.at[0], h_r.at[0], (mate, v, g))
    send(hb.at[c, my_pos], hb.at[c, my_pos], h_s.at[1], h_r.at[1], core_mate)


    wait(st.at[1], t_r.at[0])
    top = jnp.maximum(st[0, 0:1, :], st[1, 0:1, :])
    mass = st[0, 1:2, :] * jnp.exp(st[0, 0:1, :] - top) + st[1, 1:2, :] * jnp.exp(st[1, 0:1, :] - top)
    sub = lax.broadcasted_iota(jnp.int32, (8, ROWS), 0)
    sb[0] = jnp.where(sub == 0, top, mass)
    loop(1, 16, lambda r: send(sb.at[0], sb.at[r], t_s.at[1], t_r.at[1], plane_dev(r, c)))
    exchange(2)

    wait(cz.at[pl.ds(0, LAST)], c_r.at[0])
    part = cz[0]
    for p in range(1, 8):
        part = part + cz[p]
    cm[0] = part
    send(cm.at[0], cm.at[1], c_s.at[1], c_r.at[1], (mate, v, g))
    exchange(3)

    wait(cm.at[1], c_r.at[1])
    sizes = jnp.sum(cm[0] + cm[1], axis=1, keepdims=True)
    own_size = jnp.sum(member * sizes, axis=0, keepdims=True)
    weight = masked * (NT * ROWS // SEGS) / own_size
    acc[...] = jnp.zeros_like(acc)

    wait(sb.at[pl.ds(1, 15)], t_r.at[1])

    def lse(first):
        top = sb[first, 0:1, :]
        for r in range(first + 1, first + 8):
            top = jnp.maximum(top, sb[r, 0:1, :])
        mass = jnp.zeros_like(top)
        for r in range(first, first + 8):
            mass = mass + sb[r, 1:2, :] * jnp.exp(sb[r, 0:1, :] - top)
        return top + jnp.log(mass)

    own_lse, other_lse = lse(0), lse(8)
    sc[...] = jnp.zeros_like(sc)
    sc[0:8, :] = jnp.where(sub == 0, own_lse, jnp.where(sub == 1, other_lse, weight))
    col[...] = sc[...].T

    sign = jnp.where(g == 0, -1.0, 1.0).astype(F32)

    def block(t, p):
        i = (z // 2 + 8 - off(p)) % 8
        first = (2 * i + c * (15 + 2 * par)) % 16
        rows = pl.ds(pl.multiple_of(TH * t, TH), TH)
        stats = col[rows, :]
        own_l, other_l, wgt = stats[:, 0:1], stats[:, 1:2], stats[:, 2:3]
        scale = (SOFTEN * sign) * wgt
        for n, k in enumerate((first, (first + 1) % 16)):
            cols = pl.ds(pl.multiple_of(BLK * k, BLK), BLK)
            own_at = pl.ds(pl.multiple_of(COLS * g + BLK * k, BLK), BLK)
            log_own = lg[rows, own_at].astype(F32) * (1.0 / SOFTEN) - own_l
            log_other = ao[rows, cols].astype(F32) * (1.0 / SOFTEN) - other_l
            p_own = jnp.exp(log_own)
            p_other = jnp.exp(log_other)
            grad = (scale * (p_own - p_other)).astype(BF16)
            term = jnp.where(g == 0, p_own, p_other) * (log_own - log_other)
            acc[...] += wgt * (term[:, :128] + term[:, 128:])
            gn[rows, cols] = grad
            gb[p, rows, BLK * n:BLK * n + BLK] = grad

    def chunk(t):
        wait(ao.at[pl.ds(pl.multiple_of(TH * t, TH), TH)], x_r.at[t])
        there = pl.ds(pl.multiple_of(16 * t, 16), 16)

        def place(p):
            block(t, p)
            for e in range(2):
                here = pl.ds(pl.multiple_of(TH * t + 16 * e, 16), 16)
                send(
                    gb.at[p, here], grx.at[c, p, there], g_s.at[0], g_r.at[2 * (t // 2) + p // 4],
                    (column(p), 2 * j + e, g),
                )

        loop(0, LAST, place)
        block(t, LAST)
        mine = pl.ds(pl.multiple_of(TH * t + 16 * c, 16), 16)
        theirs = pl.ds(pl.multiple_of(TH * t + 16 * oc, 16), 16)
        grx[c, LAST, there, :] = gb[LAST, mine, :]
        send(gb.at[LAST, theirs], grx.at[c, LAST, there], g_s.at[1], g_r.at[4 + t // 2], core_mate)

    loop(0, 4, chunk)

    out_own = pltpu.make_async_copy(gn, grad_out, s_loc.at[4])
    out_own.start()

    lp[0] = (acc[0:8] + acc[8:16] + acc[16:24] + acc[24:32]) * (-sign)
    loop(1, 16, lambda r: send(lp.at[0], lp.at[r], l_s.at[2], l_r.at[2], plane_dev(r, c)))

    wait(hb.at[c, 1 - my_pos], h_r.at[0])
    send(hb.at[c, 1 - my_pos], hb.at[c, 1 - my_pos], h_s.at[2], h_r.at[2], core_mate)

    out_row = lax.broadcasted_iota(jnp.int32, (128, 128), 0)
    in_row = lax.broadcasted_iota(jnp.int32, (128, 128), 1)
    source = ((out_row // 4) % 4) * TH + (out_row // 16) * 4 + out_row % 4
    order = (in_row == source).astype(F32).astype(BF16)

    wait(hb.at[oc, (z + oc) % 2], h_r.at[1])
    wait(hb.at[oc, 1 - (z + oc) % 2], h_r.at[2])

    def loss_plane():
        wait(lp.at[pl.ds(1, 15)], l_r.at[2])
        part = lp[0]
        for r in range(1, 16):
            part = part + lp[r]
        lc[0] = part
        send(lc.at[0], lc.at[1], l_s.at[3], l_r.at[3], core_mate)

    def reduce(q):
        wait(rb.at[q, pl.ds(1, 15)], p_r.at[q])
        total = pb[q, g, j].astype(F32)
        for r in range(1, 16):
            total = total + rb[q, r].astype(F32)
        rsum[q] = total

    def multiply(q):
        th, bh = q // 2, q % 2
        rows = pl.ds(pl.multiple_of(TH * th, TH), TH)

        @pl.when(bh == 0)
        def _():
            wait(grx.at[:, pl.ds(0, 4), rows], g_r.at[2 * th])

        @pl.when(bh == 1)
        def _():
            wait(grx.at[:, pl.ds(4, 3), rows], g_r.at[2 * th + 1])
            wait(grx.at[oc, LAST, rows], g_r.at[4 + th])

        xs = []
        for b in range(2):
            x = grx[b, pl.ds(4 * bh, 4), rows, :].reshape(128, 2 * BLK)
            xs.append(jnp.dot(order, x, preferred_element_type=F32).astype(BF16))
        for gg in range(2):
            part = jnp.dot(
                xs[0], hb[0, :, :, HH * gg:HH * gg + HH].reshape(512, HH), preferred_element_type=F32
            ) + jnp.dot(
                xs[1], hb[1, :, :, HH * gg:HH * gg + HH].reshape(512, HH), preferred_element_type=F32
            )
            pb[q, gg] = part.astype(BF16).reshape(8, 16, HH)

        def share(r):
            j2, g2 = plane(r)
            send(pb.at[q, g2, j2], rb.at[q, r], p_s.at[q], p_r.at[q], (z, j2 * 2 + c, g2))

        loop(1, 16, share)

        @pl.when(q > 0)
        def _():
            reduce(q - 1)

        pl.when(q == 1)(loss_plane)

    def spread(bh):
        for bb in range(4):
            p = 4 * bh + bb
            x = jnp.concatenate([rsum[bh, 4 * bb:4 * bb + 4], rsum[2 + bh, 4 * bb:4 * bb + 4]], axis=0)
            x = jnp.concatenate([x[:, :512], jnp.pad(x[:, 512:], ((0, 0), (0, 128)))], axis=0)
            if p == LAST:
                own[...] = x
            else:
                zs[p] = x.astype(BF16)
                send(zs.at[p], zr.at[p], z_s.at[bh], z_r.at[bh], ((z + 2 * off(p)) % NT, v, g))

    loop(0, 4, multiply)
    spread(0)
    wait(lc.at[1], l_r.at[3])
    lz[LAST] = lc[0] + lc[1]
    loop(0, LAST, lambda p: send(lz.at[LAST], lz.at[p], l_s.at[0], l_r.at[0], (column(p), v, g)))
    reduce(3)
    spread(1)

    wait(zr.at[pl.ds(0, 4)], z_r.at[0])
    wait(zr.at[pl.ds(4, 3)], z_r.at[1])
    total = own[...]
    for p in range(LAST):
        total = total + zr[p].astype(F32)
    slot = 8 * c + j
    fb[slot] = jnp.concatenate([total[:8], total[8:, :384]], axis=1)
    loop(1, 8, lambda r: send(fb.at[slot], fb.at[slot], f_s, f_r, plane_dev(r, c)))
    loop(0, 8, lambda r: send(fb.at[slot], fb.at[slot], f_s, f_r, plane_dev(r, oc)))

    wait(lz.at[pl.ds(0, LAST)], l_r.at[0])
    part = lz[0]
    for p in range(1, 8):
        part = part + lz[p]
    lm[0] = part
    send(lm.at[0], lm.at[1], l_s.at[1], l_r.at[1], (mate, v, g))

    loop(0, 4, lambda t: wait(ao.at[pl.ds(0, TH)], x_s.at[t]))
    wait(grx.at[:, pl.ds(0, LAST)], g_s.at[0])
    wait(grx.at[0, LAST], g_s.at[1])
    loop(0, 3, lambda k: wait(hb.at[0, 0], h_s.at[k]))
    wait(cz.at[pl.ds(0, LAST)], c_s.at[0])
    wait(cm.at[1], c_s.at[1])
    wait(st.at[1], t_s.at[0])
    wait(sb.at[pl.ds(1, 15)], t_s.at[1])
    out_own.wait()
    loop(0, 4, lambda q: wait(rb.at[q, pl.ds(1, 15)], p_s.at[q]))
    wait(zr.at[pl.ds(0, 4)], z_s.at[0])
    wait(zr.at[pl.ds(4, 3)], z_s.at[1])
    wait(lz.at[pl.ds(0, LAST)], l_s.at[0])
    wait(lm.at[1], l_s.at[1])
    wait(lp.at[pl.ds(1, 15)], l_s.at[2])
    wait(lc.at[1], l_s.at[3])
    wait(lm.at[1], l_r.at[1])
    loss_out[...] = jnp.sum(lm[0] + lm[1], keepdims=True) * (SOFTEN * SOFTEN) / (NT * ROWS)

    wait(fb.at[pl.ds(0, 15)], f_r)
    for t in range(4):
        for e in range(2):
            for h in range(2):
                n = 8 * e + 4 * (t % 2) + 2 * h
                at = 4 * (t // 2)
                row = TH * t + 16 * e + 8 * h
                hid_out[row:row + 8, :] = jnp.concatenate(
                    [fb[n, at:at + 4], fb[n + 1, at:at + 4]], axis=0
                )
    wait(fb.at[pl.ds(0, 15)], f_s)


def per_device(logits, segment_ids, token_mask, student_head):
    dma = pltpu.SemaphoreType.DMA
    any_space = pl.BlockSpec(memory_space=pl.ANY)
    vmem_space = pl.BlockSpec(memory_space=pltpu.VMEM)
    grad, hidden, loss = pl.pallas_call(
        kernel,
        out_shape=(
            jax.ShapeDtypeStruct((ROWS, COLS), BF16),
            jax.ShapeDtypeStruct((ROWS, HH), F32),
            jax.ShapeDtypeStruct((1, 1), F32),
        ),
        in_specs=[any_space] * 4,
        out_specs=(any_space, vmem_space, vmem_space),
        scratch_shapes=[
            pltpu.VMEM((ROWS, 2 * COLS), BF16),
            pltpu.VMEM((ROWS, COLS), BF16),
            pltpu.VMEM((8, ROWS, 2 * BLK), BF16),
            pltpu.VMEM((ROWS, COLS), BF16),
            pltpu.VMEM((2, 8, HALF, 2 * BLK), BF16),
            pltpu.VMEM((2, 2, BLK, HS), BF16),
            pltpu.VMEM((4, 2, 8, 16, HH), BF16),
            pltpu.VMEM((4, 16, 16, HH), BF16),
            pltpu.VMEM((4, 16, HH), F32),
            pltpu.VMEM((LAST, 16, 512), BF16),
            pltpu.VMEM((LAST, 16, 512), BF16),
            pltpu.VMEM((16, 512), F32),
            pltpu.VMEM((16, 8, HH), F32),
            pltpu.VMEM((128, 128), F32),
            pltpu.VMEM((128, 128), F32),
            pltpu.VMEM((2, 8, 128), F32),
            pltpu.VMEM((16, 8, 128), F32),
            pltpu.VMEM((8, 8, 128), F32),
            pltpu.VMEM((2, 8, 128), F32),
            pltpu.VMEM((TH, 128), F32),
            pltpu.VMEM((8, 8, 128), F32),
            pltpu.VMEM((2, 8, 128), F32),
            pltpu.VMEM((16, 8, 128), F32),
            pltpu.VMEM((2, 8, 128), F32),
            pltpu.VMEM((1, ROWS), jnp.int32),
            pltpu.VMEM((1, ROWS), jnp.int32),
            dma((5,)),
            dma((4,)), dma((4,)),
            dma((3,)), dma((3,)),
            dma((2,)), dma((2,)),
            dma((2,)), dma((2,)),
            dma((2,)), dma((6,)),
            dma((4,)), dma((4,)),
            dma((2,)), dma((2,)),
            dma, dma,
            dma((4,)), dma((4,)),
        ],
        compiler_params=pltpu.CompilerParams(
            collective_id=0, has_side_effects=True, vmem_limit_bytes=VMEM_BYTES
        ),
        cost_estimate=pl.CostEstimate(
            flops=2 * ROWS * COLS * HS, bytes_accessed=6 * 1024 * 1024, transcendentals=3 * ROWS * COLS
        ),
        name="distill",
    )(
        logits.reshape(ROWS, 2 * COLS),
        segment_ids.reshape(1, ROWS),
        token_mask.reshape(1, ROWS),
        student_head.reshape(BLK, HS),
    )
    return grad, hidden, loss.reshape(())


def solution(mesh):
    placed = (P("grp", "tok", "vocab"), P("tok"), P("tok"), P(("vocab", "grp"), "tok", None, None))
    return jax.shard_map(
        per_device,
        mesh=mesh,
        in_specs=placed,
        out_specs=(P("tok", ("vocab", "grp")), P("tok", "grp"), P()),
        check_vma=False,
    )
```

```python
import jax
import jax.numpy as jnp
from jax import lax
from jax.experimental import pallas as pl
from jax.experimental.pallas import tpu as pltpu
from jax.sharding import PartitionSpec as P

SEGS = 8
SOFTEN = 2.0
NT = 16
ROWS = 128
HALF = 64
TH = 32
BLK = 256
COLS = 4096
HS = 1792
HH = 896
VMEM_BYTES = 54 * 1024 * 1024
MESH = pl.DeviceIdType.MESH
F32 = jnp.float32
BF16 = jnp.bfloat16
LAST = 7


def rem(a, b):
    return lax.rem(jnp.int32(a), jnp.int32(b))


def div(a, b):
    return lax.div(jnp.int32(a), jnp.int32(b))


def off(p):
    return rem(4 + div(p + 1, 2) * (1 - 2 * rem(p, 2)), 8)


def kernel(
    lg_hbm, seg_hbm, mask_hbm, head_hbm,
    grad_out, hid_out, loss_out,
    lg, ao, gb, gn, grx, hb, pb, rb, rsum, zs, zr, own, fb,
    sc, col, st, sb, cz, cm, acc, lz, lm, lp, lc, seg_ref, mask_ref,
    s_loc, x_s, x_r, h_s, h_r, c_s, c_r, t_s, t_r, g_s, g_r,
    p_s, p_r, z_s, z_r, f_s, f_r, l_s, l_r,
):
    z = lax.axis_index("tok")
    v = lax.axis_index("vocab")
    g = lax.axis_index("grp")
    c = rem(v, 2)
    xl = rem(div(v, 2), 2)
    y = div(v, 4)
    j = div(v, 2)
    par = rem(z, 2)
    oc = 1 - c
    og = 1 - g
    ov = v + 1 - 2 * c
    mate = rem(z + 1 + 14 * rem(z + c, 2), NT)
    my_pos = rem(z + c, 2)

    def plane(r):
        h, a, b = div(r, 8), rem(div(r, 2), 4), rem(r, 2)
        y2 = rem(y + 4 - a, 4)
        x2 = rem(xl + 2 - b, 2)
        g2 = rem(g + 2 - h, 2)
        return y2 * 2 + x2, g2

    def plane_dev(r, core):
        j2, g2 = plane(r)
        return (z, j2 * 2 + core, g2)

    def column(p):
        return rem(z + NT - 2 * off(p), NT)

    def send(src, dst, ss, rs, dev):
        copy = pltpu.make_async_remote_copy(
            src_ref=src, dst_ref=dst, send_sem=ss, recv_sem=rs, device_id=dev, device_id_type=MESH
        )
        copy.start()

    def wait(ref, sem):
        pltpu.make_async_copy(ref, ref, sem).wait()

    def loop(first, last, body):
        def step(i, carry):
            body(i)
            return carry

        lax.fori_loop(first, last, step, 0)

    core_mate = (z, ov, g)

    in_logits = pltpu.make_async_copy(lg_hbm, lg, s_loc.at[0])
    in_logits.start()
    in_head = pltpu.make_async_copy(head_hbm, hb.at[c, my_pos], s_loc.at[1])
    in_head.start()
    in_seg = pltpu.make_async_copy(seg_hbm, seg_ref, s_loc.at[2])
    in_seg.start()
    in_mask = pltpu.make_async_copy(mask_hbm, mask_ref, s_loc.at[3])
    in_mask.start()

    barrier = pltpu.get_barrier_semaphore()

    def greet(dev):
        pl.semaphore_signal(barrier, inc=1, device_id=dev, device_id_type=MESH)

    greet((mate, v, g))
    loop(1, 16, lambda r: greet(plane_dev(r, c)))
    loop(0, 8, lambda r: greet(plane_dev(r, oc)))

    def greet_column(p):
        greet((column(p), v, g))
        greet((column(p), ov, g))

    loop(0, LAST, greet_column)

    in_logits.wait()
    lane = lax.broadcasted_iota(jnp.int32, (16, 128), 1)

    def stat_rows(i):
        rows = pl.ds(pl.multiple_of(i * 16, 16), 16)
        top = jnp.max(lg[rows, :].astype(F32), axis=1, keepdims=True) * (1.0 / SOFTEN)
        mass = jnp.sum(
            jnp.exp(lg[rows, :].astype(F32) * (1.0 / SOFTEN) - top), axis=1, keepdims=True
        )
        sc[rows, :] = jnp.where(lane == 0, top, mass)

    loop(0, ROWS // 16, stat_rows)
    st[0] = sc[...].T[:8]
    pl.semaphore_wait(barrier, 38)

    other_cols = pl.ds(pl.multiple_of(COLS * og, COLS), COLS)

    def exchange(t):
        rows = pl.ds(pl.multiple_of(TH * t, TH), TH)
        send(lg_hbm.at[rows, other_cols], ao.at[rows], x_s.at[t], x_r.at[t], (z, v, og))

    send(st.at[0], st.at[1], t_s.at[0], t_r.at[0], core_mate)
    exchange(0)

    in_seg.wait()
    in_mask.wait()
    docs = lax.broadcasted_iota(jnp.int32, (SEGS, ROWS), 0)
    member = (seg_ref[...] == docs).astype(F32)
    masked = mask_ref[...].astype(F32)
    cz[LAST] = member * masked
    loop(0, LAST, lambda p: send(cz.at[LAST], cz.at[p], c_s.at[0], c_r.at[0], (column(p), v, g)))

    in_head.wait()
    send(hb.at[c, my_pos], hb.at[c, my_pos], h_s.at[0], h_r.at[0], (mate, v, g))
    send(hb.at[c, my_pos], hb.at[c, my_pos], h_s.at[1], h_r.at[1], core_mate)


    wait(st.at[1], t_r.at[0])
    top = jnp.maximum(st[0, 0:1, :], st[1, 0:1, :])
    mass = st[0, 1:2, :] * jnp.exp(st[0, 0:1, :] - top) + st[1, 1:2, :] * jnp.exp(st[1, 0:1, :] - top)
    sub = lax.broadcasted_iota(jnp.int32, (8, ROWS), 0)
    sb[0] = jnp.where(sub == 0, top, mass)
    loop(1, 16, lambda r: send(sb.at[0], sb.at[r], t_s.at[1], t_r.at[1], plane_dev(r, c)))
    exchange(1)

    wait(cz.at[pl.ds(0, LAST)], c_r.at[0])
    part = cz[0]
    for p in range(1, 8):
        part = part + cz[p]
    cm[0] = part
    send(cm.at[0], cm.at[1], c_s.at[1], c_r.at[1], (mate, v, g))

    wait(cm.at[1], c_r.at[1])
    sizes = jnp.sum(cm[0] + cm[1], axis=1, keepdims=True)
    own_size = jnp.sum(member * sizes, axis=0, keepdims=True)
    weight = masked * (NT * ROWS // SEGS) / own_size
    acc[...] = jnp.zeros_like(acc)

    wait(sb.at[pl.ds(1, 15)], t_r.at[1])

    def lse(first):
        top = sb[first, 0:1, :]
        for r in range(first + 1, first + 8):
            top = jnp.maximum(top, sb[r, 0:1, :])
        mass = jnp.zeros_like(top)
        for r in range(first, first + 8):
            mass = mass + sb[r, 1:2, :] * jnp.exp(sb[r, 0:1, :] - top)
        return top + jnp.log(mass)

    own_lse, other_lse = lse(0), lse(8)
    sc[...] = jnp.zeros_like(sc)
    sc[0:8, :] = jnp.where(sub == 0, own_lse, jnp.where(sub == 1, other_lse, weight))
    col[...] = sc[...].T

    sign = jnp.where(g == 0, -1.0, 1.0).astype(F32)

    def block(t, p):
        i = rem(div(z, 2) + 8 - off(p), 8)
        first = rem(2 * i + c * (15 + 2 * par), 16)
        rows = pl.ds(pl.multiple_of(TH * t, TH), TH)
        stats = col[rows, :]
        own_l, other_l, wgt = stats[:, 0:1], stats[:, 1:2], stats[:, 2:3]
        scale = (SOFTEN * sign) * wgt
        for n, k in enumerate((first, rem(first + 1, 16))):
            cols = pl.ds(pl.multiple_of(BLK * k, BLK), BLK)
            own_at = pl.ds(pl.multiple_of(COLS * g + BLK * k, BLK), BLK)
            log_own = lg[rows, own_at].astype(F32) * (1.0 / SOFTEN) - own_l
            log_other = ao[rows, cols].astype(F32) * (1.0 / SOFTEN) - other_l
            p_own = jnp.exp(log_own)
            p_other = jnp.exp(log_other)
            grad = (scale * (p_own - p_other)).astype(BF16)
            term = jnp.where(g == 0, p_own, p_other) * (log_own - log_other)
            acc[...] += wgt * (term[:, :128] + term[:, 128:])
            gn[rows, cols] = grad
            gb[p, rows, BLK * n:BLK * n + BLK] = grad

    def chunk(t):
        wait(ao.at[pl.ds(pl.multiple_of(TH * t, TH), TH)], x_r.at[t])
        pl.when(t < 2)(lambda: exchange(t + 2))
        there = pl.ds(pl.multiple_of(16 * t, 16), 16)

        def place(p):
            block(t, p)
            pl.when(t < 2)(lambda: ship_block(t, p))

        loop(0, LAST, place)
        block(t, LAST)
        mine = pl.ds(pl.multiple_of(TH * t + 16 * c, 16), 16)
        theirs = pl.ds(pl.multiple_of(TH * t + 16 * oc, 16), 16)
        grx[c, LAST, there, :] = gb[LAST, mine, :]
        send(gb.at[LAST, theirs], grx.at[c, LAST, there], g_s.at[4 + t], g_r.at[4 + t], core_mate)

    def ship_block(t, p):
        there = pl.ds(pl.multiple_of(16 * t, 16), 16)
        for e in range(2):
            here = pl.ds(pl.multiple_of(TH * t + 16 * e, 16), 16)
            send(
                gb.at[p, here], grx.at[c, p, there], g_s.at[t], g_r.at[t], (column(p), 2 * j + e, g)
            )

    loop(0, 4, chunk)

    out_own = pltpu.make_async_copy(gn, grad_out, s_loc.at[4])
    out_own.start()

    lp[0] = (acc[0:8] + acc[8:16] + acc[16:24] + acc[24:32]) * (-sign)
    loop(1, 16, lambda r: send(lp.at[0], lp.at[r], l_s.at[2], l_r.at[2], plane_dev(r, c)))

    wait(hb.at[c, 1 - my_pos], h_r.at[0])
    send(hb.at[c, 1 - my_pos], hb.at[c, 1 - my_pos], h_s.at[2], h_r.at[2], core_mate)

    out_row = lax.broadcasted_iota(jnp.int32, (128, 128), 0)
    in_row = lax.broadcasted_iota(jnp.int32, (128, 128), 1)
    source = ((out_row // 2) % 8) * 16 + (out_row // 16) * 2 + out_row % 2
    order = (in_row == source).astype(F32).astype(BF16)

    wait(hb.at[oc, rem(z + oc, 2)], h_r.at[1])
    wait(hb.at[oc, 1 - rem(z + oc, 2)], h_r.at[2])

    def loss_plane():
        wait(lp.at[pl.ds(1, 15)], l_r.at[2])
        part = lp[0]
        for r in range(1, 16):
            part = part + lp[r]
        lc[0] = part
        send(lc.at[0], lc.at[1], l_s.at[3], l_r.at[3], core_mate)

    def reduce(q):
        wait(rb.at[q, pl.ds(1, 15)], p_r.at[q])
        total = pb[q, g, j].astype(F32)
        for r in range(1, 16):
            total = total + rb[q, r].astype(F32)
        rsum[q] = total

    def multiply(q):
        rows = pl.ds(pl.multiple_of(16 * q, 16), 16)

        @pl.when(q < 2)
        def _():
            wait(grx.at[:, pl.ds(0, LAST), rows], g_s.at[q])
            loop(0, LAST, lambda p: ship_block(q + 2, p))

        wait(grx.at[:, pl.ds(0, LAST), rows], g_r.at[q])
        wait(grx.at[oc, LAST, rows], g_r.at[4 + q])
        xs = []
        for b in range(2):
            x = grx[b, :, rows, :].reshape(128, 2 * BLK)
            xs.append(jnp.dot(order, x, preferred_element_type=F32).astype(BF16))
        def share(r):
            j2, g2 = plane(r)
            send(pb.at[q, g2, j2], rb.at[q, r], p_s.at[q], p_r.at[q], (z, j2 * 2 + c, g2))

        for gg, first, last in ((og, 8, 16), (g, 1, 8)):
            cols = pl.ds(pl.multiple_of(HH * gg, 128), HH)
            part = jnp.dot(
                xs[0], hb[0, :, :, cols].reshape(512, HH), preferred_element_type=F32
            ) + jnp.dot(xs[1], hb[1, :, :, cols].reshape(512, HH), preferred_element_type=F32)
            pb[q, gg] = part.astype(BF16).reshape(8, 16, HH)
            loop(first, last, share)

        @pl.when(q > 0)
        def _():
            reduce(q - 1)

        pl.when(q == 1)(loss_plane)

        @pl.when(q == 3)
        def _():
            for done in range(3):
                pack(done)
            spread(0, 3, 0)

    def pack(q):
        for p in range(8):
            pair = rsum[q, 2 * p:2 * p + 2]
            x = jnp.concatenate(
                [pair[:, 128 * k:128 * k + 128] for k in range(7)] + [jnp.zeros((2, 128), F32)], axis=0
            )
            if p == LAST:
                own[:, 128 * q:128 * q + 128] = x
            else:
                zs[p, :, 128 * q:128 * q + 128] = x.astype(BF16)

    def spread(first, last, k):
        cols = slice(128 * first, 128 * last)
        for p in range(LAST):
            send(
                zs.at[p, :, cols], zr.at[p, :, cols], z_s.at[k], z_r.at[k],
                (rem(z + 2 * off(p), NT), v, g),
            )

    loop(0, 4, multiply)
    wait(lc.at[1], l_r.at[3])
    lz[LAST] = lc[0] + lc[1]
    loop(0, LAST, lambda p: send(lz.at[LAST], lz.at[p], l_s.at[0], l_r.at[0], (column(p), v, g)))
    reduce(3)
    pack(3)
    spread(3, 4, 1)

    wait(zr.at[:, :, 0:384], z_r.at[0])
    wait(zr.at[:, :, 384:512], z_r.at[1])
    total = own[...]
    for p in range(LAST):
        total = total + zr[p].astype(F32)
    slot = 8 * c + j
    fb[slot] = total
    loop(1, 8, lambda r: send(fb.at[slot], fb.at[slot], f_s, f_r, plane_dev(r, c)))
    loop(0, 8, lambda r: send(fb.at[slot], fb.at[slot], f_s, f_r, plane_dev(r, oc)))

    wait(lz.at[pl.ds(0, LAST)], l_r.at[0])
    part = lz[0]
    for p in range(1, 8):
        part = part + lz[p]
    lm[0] = part
    send(lm.at[0], lm.at[1], l_s.at[1], l_r.at[1], (mate, v, g))

    loop(0, 4, lambda t: wait(ao.at[pl.ds(0, TH)], x_s.at[t]))
    for t in range(4):
        rows = pl.ds(16 * t, 16)
        if t >= 2:
            wait(grx.at[:, pl.ds(0, LAST), rows], g_s.at[t])
        wait(grx.at[0, LAST, rows], g_s.at[4 + t])
    loop(0, 3, lambda k: wait(hb.at[0, 0], h_s.at[k]))
    wait(cz.at[pl.ds(0, LAST)], c_s.at[0])
    wait(cm.at[1], c_s.at[1])
    wait(st.at[1], t_s.at[0])
    wait(sb.at[pl.ds(1, 15)], t_s.at[1])
    out_own.wait()
    loop(0, 4, lambda q: wait(rb.at[q, pl.ds(1, 15)], p_s.at[q]))
    wait(zr.at[:, :, 0:384], z_s.at[0])
    wait(zr.at[:, :, 384:512], z_s.at[1])
    wait(lz.at[pl.ds(0, LAST)], l_s.at[0])
    wait(lm.at[1], l_s.at[1])
    wait(lp.at[pl.ds(1, 15)], l_s.at[2])
    wait(lc.at[1], l_s.at[3])
    wait(lm.at[1], l_r.at[1])
    loss_out[...] = jnp.sum(lm[0] + lm[1], keepdims=True) * (SOFTEN * SOFTEN) / (NT * ROWS)

    wait(fb.at[pl.ds(0, 15)], f_r)
    for t in range(4):
        for e in range(2):
            for h in range(2):
                n = 8 * e + 4 * h
                row = TH * t + 16 * e + 8 * h
                for k in range(7):
                    hid_out[row:row + 8, 128 * k:128 * k + 128] = jnp.concatenate(
                        [fb[n + i, 2 * k:2 * k + 2, 128 * t:128 * t + 128] for i in range(4)], axis=0
                    )
    wait(fb.at[pl.ds(0, 15)], f_s)


def per_device(logits, segment_ids, token_mask, student_head):
    dma = pltpu.SemaphoreType.DMA
    any_space = pl.BlockSpec(memory_space=pl.ANY)
    vmem_space = pl.BlockSpec(memory_space=pltpu.VMEM)
    grad, hidden, loss = pl.pallas_call(
        kernel,
        out_shape=(
            jax.ShapeDtypeStruct((ROWS, COLS), BF16),
            jax.ShapeDtypeStruct((ROWS, HH), F32),
            jax.ShapeDtypeStruct((1, 1), F32),
        ),
        in_specs=[any_space] * 4,
        out_specs=(any_space, vmem_space, vmem_space),
        scratch_shapes=[
            pltpu.VMEM((ROWS, 2 * COLS), BF16),
            pltpu.VMEM((ROWS, COLS), BF16),
            pltpu.VMEM((8, ROWS, 2 * BLK), BF16),
            pltpu.VMEM((ROWS, COLS), BF16),
            pltpu.VMEM((2, 8, HALF, 2 * BLK), BF16),
            pltpu.VMEM((2, 2, BLK, HS), BF16),
            pltpu.VMEM((4, 2, 8, 16, HH), BF16),
            pltpu.VMEM((4, 16, 16, HH), BF16),
            pltpu.VMEM((4, 16, HH), F32),
            pltpu.VMEM((LAST, 16, 512), BF16),
            pltpu.VMEM((LAST, 16, 512), BF16),
            pltpu.VMEM((16, 512), F32),
            pltpu.VMEM((16, 16, 512), F32),
            pltpu.VMEM((128, 128), F32),
            pltpu.VMEM((128, 128), F32),
            pltpu.VMEM((2, 8, 128), F32),
            pltpu.VMEM((16, 8, 128), F32),
            pltpu.VMEM((8, 8, 128), F32),
            pltpu.VMEM((2, 8, 128), F32),
            pltpu.VMEM((TH, 128), F32),
            pltpu.VMEM((8, 8, 128), F32),
            pltpu.VMEM((2, 8, 128), F32),
            pltpu.VMEM((16, 8, 128), F32),
            pltpu.VMEM((2, 8, 128), F32),
            pltpu.VMEM((1, ROWS), jnp.int32),
            pltpu.VMEM((1, ROWS), jnp.int32),
            dma((5,)),
            dma((4,)), dma((4,)),
            dma((3,)), dma((3,)),
            dma((2,)), dma((2,)),
            dma((2,)), dma((2,)),
            dma((8,)), dma((8,)),
            dma((4,)), dma((4,)),
            dma((2,)), dma((2,)),
            dma, dma,
            dma((4,)), dma((4,)),
        ],
        compiler_params=pltpu.CompilerParams(
            collective_id=0, has_side_effects=True, vmem_limit_bytes=VMEM_BYTES
        ),
        cost_estimate=pl.CostEstimate(
            flops=2 * ROWS * COLS * HS, bytes_accessed=6 * 1024 * 1024, transcendentals=3 * ROWS * COLS
        ),
        name="distill",
    )(
        logits.reshape(ROWS, 2 * COLS),
        segment_ids.reshape(1, ROWS),
        token_mask.reshape(1, ROWS),
        student_head.reshape(BLK, HS),
    )
    return grad, hidden, loss.reshape(())


def solution(mesh):
    placed = (P("grp", "tok", "vocab"), P("tok"), P("tok"), P(("vocab", "grp"), "tok", None, None))
    return jax.shard_map(
        per_device,
        mesh=mesh,
        in_specs=placed,
        out_specs=(P("tok", ("vocab", "grp")), P("tok", "grp"), P()),
        check_vma=False,
    )
```

```python
import jax
import jax.numpy as jnp
from jax import lax
from jax.experimental import pallas as pl
from jax.experimental.pallas import tpu as pltpu
from jax.sharding import PartitionSpec as P

SEGS = 8
SOFTEN = 2.0
NT = 16
ROWS = 128
HALF = 64
TH = 32
BLK = 256
COLS = 4096
HS = 1792
HH = 896
VMEM_BYTES = 54 * 1024 * 1024
MESH = pl.DeviceIdType.MESH
F32 = jnp.float32
BF16 = jnp.bfloat16
LAST = 7


def rem(a, b):
    return lax.rem(jnp.int32(a), jnp.int32(b))


def div(a, b):
    return lax.div(jnp.int32(a), jnp.int32(b))


def off(p):
    return rem(4 + div(p + 1, 2) * (1 - 2 * rem(p, 2)), 8)


def kernel(
    lg_hbm, seg_hbm, mask_hbm, head_hbm,
    grad_out, hid_out, loss_out,
    lg, ao, gb, gn, grx, hb, pb, rb, rsum, zs, zr, own, fb,
    sc, col, st, sb, cz, cm, acc, lz, lm, lp, lc, seg_ref, mask_ref,
    s_loc, x_s, x_r, h_s, h_r, c_s, c_r, t_s, t_r, g_s, g_r,
    p_s, p_r, z_s, z_r, f_s, f_r, l_s, l_r,
):
    z = lax.axis_index("tok")
    v = lax.axis_index("vocab")
    g = lax.axis_index("grp")
    c = rem(v, 2)
    xl = rem(div(v, 2), 2)
    y = div(v, 4)
    j = div(v, 2)
    par = rem(z, 2)
    oc = 1 - c
    og = 1 - g
    ov = v + 1 - 2 * c
    mate = rem(z + 1 + 14 * rem(z + c, 2), NT)
    my_pos = rem(z + c, 2)

    def plane(r):
        h, a, b = div(r, 8), rem(div(r, 2), 4), rem(r, 2)
        y2 = rem(y + 4 - a, 4)
        x2 = rem(xl + 2 - b, 2)
        g2 = rem(g + 2 - h, 2)
        return y2 * 2 + x2, g2

    def plane_dev(r, core):
        j2, g2 = plane(r)
        return (z, j2 * 2 + core, g2)

    def column(p):
        return rem(z + NT - 2 * off(p), NT)

    def send(src, dst, ss, rs, dev):
        copy = pltpu.make_async_remote_copy(
            src_ref=src, dst_ref=dst, send_sem=ss, recv_sem=rs, device_id=dev, device_id_type=MESH
        )
        copy.start()

    def wait(ref, sem):
        pltpu.make_async_copy(ref, ref, sem).wait()

    def loop(first, last, body):
        def step(i, carry):
            body(i)
            return carry

        lax.fori_loop(first, last, step, 0)

    core_mate = (z, ov, g)

    in_logits = pltpu.make_async_copy(lg_hbm, lg, s_loc.at[0])
    in_logits.start()
    in_head = pltpu.make_async_copy(head_hbm, hb.at[c, my_pos], s_loc.at[1])
    in_head.start()
    in_seg = pltpu.make_async_copy(seg_hbm, seg_ref, s_loc.at[2])
    in_seg.start()
    in_mask = pltpu.make_async_copy(mask_hbm, mask_ref, s_loc.at[3])
    in_mask.start()

    barrier = pltpu.get_barrier_semaphore()

    def greet(dev):
        pl.semaphore_signal(barrier, inc=1, device_id=dev, device_id_type=MESH)

    greet((mate, v, g))
    loop(1, 16, lambda r: greet(plane_dev(r, c)))
    loop(0, 8, lambda r: greet(plane_dev(r, oc)))

    def greet_column(p):
        greet((column(p), v, g))
        greet((column(p), ov, g))

    loop(0, LAST, greet_column)

    in_logits.wait()
    lane = lax.broadcasted_iota(jnp.int32, (16, 128), 1)

    def stat_rows(i):
        rows = pl.ds(pl.multiple_of(i * 16, 16), 16)
        top = jnp.max(lg[rows, :].astype(F32), axis=1, keepdims=True) * (1.0 / SOFTEN)
        mass = jnp.sum(
            jnp.exp(lg[rows, :].astype(F32) * (1.0 / SOFTEN) - top), axis=1, keepdims=True
        )
        sc[rows, :] = jnp.where(lane == 0, top, mass)

    loop(0, ROWS // 16, stat_rows)
    st[0] = sc[...].T[:8]
    pl.semaphore_wait(barrier, 38)

    other_cols = pl.ds(pl.multiple_of(COLS * og, COLS), COLS)

    def exchange(t):
        rows = pl.ds(pl.multiple_of(TH * t, TH), TH)
        send(lg_hbm.at[rows, other_cols], ao.at[rows], x_s.at[t], x_r.at[t], (z, v, og))

    send(st.at[0], st.at[1], t_s.at[0], t_r.at[0], core_mate)
    exchange(0)

    in_seg.wait()
    in_mask.wait()
    docs = lax.broadcasted_iota(jnp.int32, (SEGS, ROWS), 0)
    member = (seg_ref[...] == docs).astype(F32)
    masked = mask_ref[...].astype(F32)
    cz[LAST] = member * masked
    loop(0, LAST, lambda p: send(cz.at[LAST], cz.at[p], c_s.at[0], c_r.at[0], (column(p), v, g)))

    in_head.wait()
    send(hb.at[c, my_pos], hb.at[c, my_pos], h_s.at[0], h_r.at[0], (mate, v, g))
    send(hb.at[c, my_pos], hb.at[c, my_pos], h_s.at[1], h_r.at[1], core_mate)


    wait(st.at[1], t_r.at[0])
    top = jnp.maximum(st[0, 0:1, :], st[1, 0:1, :])
    mass = st[0, 1:2, :] * jnp.exp(st[0, 0:1, :] - top) + st[1, 1:2, :] * jnp.exp(st[1, 0:1, :] - top)
    sub = lax.broadcasted_iota(jnp.int32, (8, ROWS), 0)
    sb[0] = jnp.where(sub == 0, top, mass)
    loop(1, 16, lambda r: send(sb.at[0], sb.at[r], t_s.at[1], t_r.at[1], plane_dev(r, c)))
    exchange(1)

    wait(cz.at[pl.ds(0, LAST)], c_r.at[0])
    part = cz[0]
    for p in range(1, 8):
        part = part + cz[p]
    cm[0] = part
    send(cm.at[0], cm.at[1], c_s.at[1], c_r.at[1], (mate, v, g))

    wait(cm.at[1], c_r.at[1])
    sizes = jnp.sum(cm[0] + cm[1], axis=1, keepdims=True)
    own_size = jnp.sum(member * sizes, axis=0, keepdims=True)
    weight = masked * (NT * ROWS // SEGS) / own_size
    acc[...] = jnp.zeros_like(acc)

    wait(sb.at[pl.ds(1, 15)], t_r.at[1])

    def lse(first):
        top = sb[first, 0:1, :]
        for r in range(first + 1, first + 8):
            top = jnp.maximum(top, sb[r, 0:1, :])
        mass = jnp.zeros_like(top)
        for r in range(first, first + 8):
            mass = mass + sb[r, 1:2, :] * jnp.exp(sb[r, 0:1, :] - top)
        return top + jnp.log(mass)

    own_lse, other_lse = lse(0), lse(8)
    sc[...] = jnp.zeros_like(sc)
    sc[0:8, :] = jnp.where(sub == 0, own_lse, jnp.where(sub == 1, other_lse, weight))
    col[...] = sc[...].T

    sign = jnp.where(g == 0, -1.0, 1.0).astype(F32)

    def block(t, p):
        i = rem(div(z, 2) + 8 - off(p), 8)
        first = rem(2 * i + c * (15 + 2 * par), 16)
        rows = pl.ds(pl.multiple_of(TH * t, TH), TH)
        stats = col[rows, :]
        own_l, other_l, wgt = stats[:, 0:1], stats[:, 1:2], stats[:, 2:3]
        scale = (SOFTEN * sign) * wgt
        for n, k in enumerate((first, rem(first + 1, 16))):
            cols = pl.ds(pl.multiple_of(BLK * k, BLK), BLK)
            own_at = pl.ds(pl.multiple_of(COLS * g + BLK * k, BLK), BLK)
            log_own = lg[rows, own_at].astype(F32) * (1.0 / SOFTEN) - own_l
            log_other = ao[rows, cols].astype(F32) * (1.0 / SOFTEN) - other_l
            p_own = jnp.exp(log_own)
            p_other = jnp.exp(log_other)
            grad = (scale * (p_own - p_other)).astype(BF16)
            term = jnp.where(g == 0, p_own, p_other) * (log_own - log_other)
            acc[...] += wgt * (term[:, :128] + term[:, 128:])
            gn[rows, cols] = grad
            gb[p, rows, BLK * n:BLK * n + BLK] = grad

    def chunk(t):
        wait(ao.at[pl.ds(pl.multiple_of(TH * t, TH), TH)], x_r.at[t])
        pl.when(t < 2)(lambda: exchange(t + 2))
        there = pl.ds(pl.multiple_of(16 * t, 16), 16)

        def place(p):
            block(t, p)
            pl.when(t < 2)(lambda: ship_block(t, p))

        loop(0, LAST, place)
        block(t, LAST)
        mine = pl.ds(pl.multiple_of(TH * t + 16 * c, 16), 16)
        theirs = pl.ds(pl.multiple_of(TH * t + 16 * oc, 16), 16)
        grx[c, LAST, there, :] = gb[LAST, mine, :]
        send(gb.at[LAST, theirs], grx.at[c, LAST, there], g_s.at[4 + t], g_r.at[4 + t], core_mate)

    def ship_block(t, p):
        there = pl.ds(pl.multiple_of(16 * t, 16), 16)
        for e in range(2):
            here = pl.ds(pl.multiple_of(TH * t + 16 * e, 16), 16)
            send(
                gb.at[p, here], grx.at[c, p, there], g_s.at[t], g_r.at[t], (column(p), 2 * j + e, g)
            )

    loop(0, 4, chunk)

    out_own = pltpu.make_async_copy(gn, grad_out, s_loc.at[4])
    out_own.start()

    lp[0] = (acc[0:8] + acc[8:16] + acc[16:24] + acc[24:32]) * (-sign)
    loop(1, 16, lambda r: send(lp.at[0], lp.at[r], l_s.at[2], l_r.at[2], plane_dev(r, c)))

    wait(hb.at[c, 1 - my_pos], h_r.at[0])
    send(hb.at[c, 1 - my_pos], hb.at[c, 1 - my_pos], h_s.at[2], h_r.at[2], core_mate)

    out_row = lax.broadcasted_iota(jnp.int32, (128, 128), 0)
    in_row = lax.broadcasted_iota(jnp.int32, (128, 128), 1)
    source = ((out_row // 2) % 8) * 16 + (out_row // 16) * 2 + out_row % 2
    order = (in_row == source).astype(F32).astype(BF16)

    wait(hb.at[oc, rem(z + oc, 2)], h_r.at[1])
    wait(hb.at[oc, 1 - rem(z + oc, 2)], h_r.at[2])

    def loss_plane():
        wait(lp.at[pl.ds(1, 15)], l_r.at[2])
        part = lp[0]
        for r in range(1, 16):
            part = part + lp[r]
        lc[0] = part
        send(lc.at[0], lc.at[1], l_s.at[3], l_r.at[3], core_mate)

    def reduce(q):
        wait(rb.at[q, pl.ds(1, 15)], p_r.at[q])
        total = pb[q, g, j].astype(F32)
        for r in range(1, 16):
            total = total + rb[q, r].astype(F32)
        rsum[q] = total

    def multiply(q):
        rows = pl.ds(pl.multiple_of(16 * q, 16), 16)

        @pl.when(q == 3)
        def _():
            reduce(2)
            for done in range(3):
                pack(done)

        @pl.when(q < 2)
        def _():
            wait(grx.at[:, pl.ds(0, LAST), rows], g_s.at[q])
            loop(0, LAST, lambda p: ship_block(q + 2, p))

        wait(grx.at[:, pl.ds(0, LAST), rows], g_r.at[q])
        wait(grx.at[oc, LAST, rows], g_r.at[4 + q])
        xs = []
        for b in range(2):
            x = grx[b, :, rows, :].reshape(128, 2 * BLK)
            xs.append(jnp.dot(order, x, preferred_element_type=F32).astype(BF16))
        def share(r):
            j2, g2 = plane(r)
            send(pb.at[q, g2, j2], rb.at[q, r], p_s.at[q], p_r.at[q], (z, j2 * 2 + c, g2))

        for gg, first, last in ((og, 8, 16), (g, 1, 8)):
            cols = pl.ds(pl.multiple_of(HH * gg, 128), HH)
            part = jnp.dot(
                xs[0], hb[0, :, :, cols].reshape(512, HH), preferred_element_type=F32
            ) + jnp.dot(xs[1], hb[1, :, :, cols].reshape(512, HH), preferred_element_type=F32)
            pb[q, gg] = part.astype(BF16).reshape(8, 16, HH)
            loop(first, last, share)

        @pl.when((q == 1) | (q == 2))
        def _():
            reduce(q - 1)

        pl.when(q == 1)(loss_plane)
        pl.when(q == 3)(lambda: spread(0, 3, 0))

    def pack(q):
        for p in range(8):
            pair = rsum[q, 2 * p:2 * p + 2]
            x = jnp.concatenate(
                [pair[:, 128 * k:128 * k + 128] for k in range(7)] + [jnp.zeros((2, 128), F32)], axis=0
            )
            if p == LAST:
                own[:, 128 * q:128 * q + 128] = x
            else:
                zs[p, :, 128 * q:128 * q + 128] = x.astype(BF16)

    def spread(first, last, k):
        cols = slice(128 * first, 128 * last)
        for p in range(LAST):
            send(
                zs.at[p, :, cols], zr.at[p, :, cols], z_s.at[k], z_r.at[k],
                (rem(z + 2 * off(p), NT), v, g),
            )

    loop(0, 4, multiply)
    wait(lc.at[1], l_r.at[3])
    lz[LAST] = lc[0] + lc[1]
    loop(0, LAST, lambda p: send(lz.at[LAST], lz.at[p], l_s.at[0], l_r.at[0], (column(p), v, g)))
    reduce(3)
    pack(3)
    spread(3, 4, 1)

    slot = 8 * c + j

    def gather(first, last, k):
        cols = slice(128 * first, 128 * last)
        wait(zr.at[:, :, cols], z_r.at[k])
        total = own[:, cols]
        for p in range(LAST):
            total = total + zr[p, :, cols].astype(F32)
        fb[slot, :, cols] = total
        mine = fb.at[slot, :, cols]
        loop(1, 8, lambda r: send(mine, mine, f_s.at[k], f_r.at[k], plane_dev(r, c)))
        loop(0, 8, lambda r: send(mine, mine, f_s.at[k], f_r.at[k], plane_dev(r, oc)))

    gather(0, 3, 0)
    gather(3, 4, 1)

    wait(lz.at[pl.ds(0, LAST)], l_r.at[0])
    part = lz[0]
    for p in range(1, 8):
        part = part + lz[p]
    lm[0] = part
    send(lm.at[0], lm.at[1], l_s.at[1], l_r.at[1], (mate, v, g))

    loop(0, 4, lambda t: wait(ao.at[pl.ds(0, TH)], x_s.at[t]))
    for t in range(4):
        rows = pl.ds(16 * t, 16)
        if t >= 2:
            wait(grx.at[:, pl.ds(0, LAST), rows], g_s.at[t])
        wait(grx.at[0, LAST, rows], g_s.at[4 + t])
    loop(0, 3, lambda k: wait(hb.at[0, 0], h_s.at[k]))
    wait(cz.at[pl.ds(0, LAST)], c_s.at[0])
    wait(cm.at[1], c_s.at[1])
    wait(st.at[1], t_s.at[0])
    wait(sb.at[pl.ds(1, 15)], t_s.at[1])
    out_own.wait()
    loop(0, 4, lambda q: wait(rb.at[q, pl.ds(1, 15)], p_s.at[q]))
    wait(zr.at[:, :, 0:384], z_s.at[0])
    wait(zr.at[:, :, 384:512], z_s.at[1])
    wait(lz.at[pl.ds(0, LAST)], l_s.at[0])
    wait(lm.at[1], l_s.at[1])
    wait(lp.at[pl.ds(1, 15)], l_s.at[2])
    wait(lc.at[1], l_s.at[3])
    wait(lm.at[1], l_r.at[1])
    loss_out[...] = jnp.sum(lm[0] + lm[1], keepdims=True) * (SOFTEN * SOFTEN) / (NT * ROWS)

    def assemble(t):
        for e in range(2):
            for h in range(2):
                n = 8 * e + 4 * h
                row = TH * t + 16 * e + 8 * h
                for k in range(7):
                    hid_out[row:row + 8, 128 * k:128 * k + 128] = jnp.concatenate(
                        [fb[n + i, 2 * k:2 * k + 2, 128 * t:128 * t + 128] for i in range(4)], axis=0
                    )

    wait(fb.at[pl.ds(0, 15), :, 0:384], f_r.at[0])
    for t in range(3):
        assemble(t)
    wait(fb.at[pl.ds(0, 15), :, 0:384], f_s.at[0])
    wait(fb.at[pl.ds(0, 15), :, 384:512], f_r.at[1])
    assemble(3)
    wait(fb.at[pl.ds(0, 15), :, 384:512], f_s.at[1])


def per_device(logits, segment_ids, token_mask, student_head):
    dma = pltpu.SemaphoreType.DMA
    any_space = pl.BlockSpec(memory_space=pl.ANY)
    vmem_space = pl.BlockSpec(memory_space=pltpu.VMEM)
    grad, hidden, loss = pl.pallas_call(
        kernel,
        out_shape=(
            jax.ShapeDtypeStruct((ROWS, COLS), BF16),
            jax.ShapeDtypeStruct((ROWS, HH), F32),
            jax.ShapeDtypeStruct((1, 1), F32),
        ),
        in_specs=[any_space] * 4,
        out_specs=(any_space, vmem_space, vmem_space),
        scratch_shapes=[
            pltpu.VMEM((ROWS, 2 * COLS), BF16),
            pltpu.VMEM((ROWS, COLS), BF16),
            pltpu.VMEM((8, ROWS, 2 * BLK), BF16),
            pltpu.VMEM((ROWS, COLS), BF16),
            pltpu.VMEM((2, 8, HALF, 2 * BLK), BF16),
            pltpu.VMEM((2, 2, BLK, HS), BF16),
            pltpu.VMEM((4, 2, 8, 16, HH), BF16),
            pltpu.VMEM((4, 16, 16, HH), BF16),
            pltpu.VMEM((4, 16, HH), F32),
            pltpu.VMEM((LAST, 16, 512), BF16),
            pltpu.VMEM((LAST, 16, 512), BF16),
            pltpu.VMEM((16, 512), F32),
            pltpu.VMEM((16, 16, 512), F32),
            pltpu.VMEM((128, 128), F32),
            pltpu.VMEM((128, 128), F32),
            pltpu.VMEM((2, 8, 128), F32),
            pltpu.VMEM((16, 8, 128), F32),
            pltpu.VMEM((8, 8, 128), F32),
            pltpu.VMEM((2, 8, 128), F32),
            pltpu.VMEM((TH, 128), F32),
            pltpu.VMEM((8, 8, 128), F32),
            pltpu.VMEM((2, 8, 128), F32),
            pltpu.VMEM((16, 8, 128), F32),
            pltpu.VMEM((2, 8, 128), F32),
            pltpu.VMEM((1, ROWS), jnp.int32),
            pltpu.VMEM((1, ROWS), jnp.int32),
            dma((5,)),
            dma((4,)), dma((4,)),
            dma((3,)), dma((3,)),
            dma((2,)), dma((2,)),
            dma((2,)), dma((2,)),
            dma((8,)), dma((8,)),
            dma((4,)), dma((4,)),
            dma((2,)), dma((2,)),
            dma((2,)), dma((2,)),
            dma((4,)), dma((4,)),
        ],
        compiler_params=pltpu.CompilerParams(
            collective_id=0, has_side_effects=True, vmem_limit_bytes=VMEM_BYTES
        ),
        cost_estimate=pl.CostEstimate(
            flops=2 * ROWS * COLS * HS, bytes_accessed=6 * 1024 * 1024, transcendentals=3 * ROWS * COLS
        ),
        name="distill",
    )(
        logits.reshape(ROWS, 2 * COLS),
        segment_ids.reshape(1, ROWS),
        token_mask.reshape(1, ROWS),
        student_head.reshape(BLK, HS),
    )
    return grad, hidden, loss.reshape(())


def solution(mesh):
    placed = (P("grp", "tok", "vocab"), P("tok"), P("tok"), P(("vocab", "grp"), "tok", None, None))
    return jax.shard_map(
        per_device,
        mesh=mesh,
        in_specs=placed,
        out_specs=(P("tok", ("vocab", "grp")), P("tok", "grp"), P()),
        check_vma=False,
    )
```

```python
import jax
import jax.numpy as jnp
from jax import lax
from jax.experimental import pallas as pl
from jax.experimental.pallas import tpu as pltpu
from jax.sharding import PartitionSpec as P

SEGS = 8
SOFTEN = 2.0
NT = 16
ROWS = 128
HALF = 64
TH = 32
BLK = 256
COLS = 4096
HS = 1792
HH = 896
VMEM_BYTES = 54 * 1024 * 1024
MESH = pl.DeviceIdType.MESH
F32 = jnp.float32
BF16 = jnp.bfloat16
LAST = 7


def rem(a, b):
    return lax.rem(jnp.int32(a), jnp.int32(b))


def div(a, b):
    return lax.div(jnp.int32(a), jnp.int32(b))


def off(p):
    return rem(4 + div(p + 1, 2) * (1 - 2 * rem(p, 2)), 8)


def kernel(
    lg_hbm, seg_hbm, mask_hbm, head_hbm,
    grad_out, hid_out, loss_out,
    lg, ao, gb, gn, grx, hb, pb, rb, rsum, zs, zr, own, fb,
    sc, col, st, sb, cz, cm, acc, lz, lm, lp, lc, seg_ref, mask_ref,
    s_loc, x_s, x_r, h_s, h_r, c_s, c_r, t_s, t_r, g_s, g_r,
    p_s, p_r, z_s, z_r, f_s, f_r, l_s, l_r,
):
    z = lax.axis_index("tok")
    v = lax.axis_index("vocab")
    g = lax.axis_index("grp")
    c = rem(v, 2)
    xl = rem(div(v, 2), 2)
    y = div(v, 4)
    j = div(v, 2)
    par = rem(z, 2)
    oc = 1 - c
    og = 1 - g
    ov = v + 1 - 2 * c
    mate = rem(z + 1 + 14 * rem(z + c, 2), NT)
    my_pos = rem(z + c, 2)

    def plane(r):
        h, a, b = div(r, 8), rem(div(r, 2), 4), rem(r, 2)
        y2 = rem(y + 4 - a, 4)
        x2 = rem(xl + 2 - b, 2)
        g2 = rem(g + 2 - h, 2)
        return y2 * 2 + x2, g2

    def plane_dev(r, core):
        j2, g2 = plane(r)
        return (z, j2 * 2 + core, g2)

    def column(p):
        return rem(z + NT - 2 * off(p), NT)

    def send(src, dst, ss, rs, dev):
        copy = pltpu.make_async_remote_copy(
            src_ref=src, dst_ref=dst, send_sem=ss, recv_sem=rs, device_id=dev, device_id_type=MESH
        )
        copy.start()

    def wait(ref, sem):
        pltpu.make_async_copy(ref, ref, sem).wait()

    def loop(first, last, body):
        def step(i, carry):
            body(i)
            return carry

        lax.fori_loop(first, last, step, 0)

    core_mate = (z, ov, g)

    in_logits = pltpu.make_async_copy(lg_hbm, lg, s_loc.at[0])
    in_logits.start()
    in_head = pltpu.make_async_copy(head_hbm, hb.at[c, my_pos], s_loc.at[1])
    in_head.start()
    in_seg = pltpu.make_async_copy(seg_hbm, seg_ref, s_loc.at[2])
    in_seg.start()
    in_mask = pltpu.make_async_copy(mask_hbm, mask_ref, s_loc.at[3])
    in_mask.start()

    barrier = pltpu.get_barrier_semaphore()

    def greet(dev):
        pl.semaphore_signal(barrier, inc=1, device_id=dev, device_id_type=MESH)

    greet((mate, v, g))
    loop(1, 16, lambda r: greet(plane_dev(r, c)))
    loop(0, 8, lambda r: greet(plane_dev(r, oc)))

    def greet_column(p):
        greet((column(p), v, g))
        greet((column(p), ov, g))

    loop(0, LAST, greet_column)

    in_logits.wait()
    lane = lax.broadcasted_iota(jnp.int32, (16, 128), 1)

    def stat_rows(i):
        rows = pl.ds(pl.multiple_of(i * 16, 16), 16)
        top = jnp.max(lg[rows, :].astype(F32), axis=1, keepdims=True) * (1.0 / SOFTEN)
        mass = jnp.sum(
            jnp.exp(lg[rows, :].astype(F32) * (1.0 / SOFTEN) - top), axis=1, keepdims=True
        )
        sc[rows, :] = jnp.where(lane == 0, top, mass)

    loop(0, ROWS // 16, stat_rows)
    st[0] = sc[...].T[:8]
    pl.semaphore_wait(barrier, 38)

    other_cols = pl.ds(pl.multiple_of(COLS * og, COLS), COLS)

    def exchange(t):
        rows = pl.ds(pl.multiple_of(TH * t, TH), TH)
        send(lg_hbm.at[rows, other_cols], ao.at[rows], x_s.at[t], x_r.at[t], (z, v, og))

    send(st.at[0], st.at[1], t_s.at[0], t_r.at[0], core_mate)
    exchange(0)

    in_seg.wait()
    in_mask.wait()
    docs = lax.broadcasted_iota(jnp.int32, (SEGS, ROWS), 0)
    member = (seg_ref[...] == docs).astype(F32)
    masked = mask_ref[...].astype(F32)
    cz[LAST] = member * masked
    loop(0, LAST, lambda p: send(cz.at[LAST], cz.at[p], c_s.at[0], c_r.at[0], (column(p), v, g)))

    in_head.wait()
    send(hb.at[c, my_pos], hb.at[c, my_pos], h_s.at[0], h_r.at[0], (mate, v, g))
    send(hb.at[c, my_pos], hb.at[c, my_pos], h_s.at[1], h_r.at[1], core_mate)


    wait(st.at[1], t_r.at[0])
    top = jnp.maximum(st[0, 0:1, :], st[1, 0:1, :])
    mass = st[0, 1:2, :] * jnp.exp(st[0, 0:1, :] - top) + st[1, 1:2, :] * jnp.exp(st[1, 0:1, :] - top)
    sub = lax.broadcasted_iota(jnp.int32, (8, ROWS), 0)
    sb[0] = jnp.where(sub == 0, top, mass)
    loop(1, 16, lambda r: send(sb.at[0], sb.at[r], t_s.at[1], t_r.at[1], plane_dev(r, c)))
    exchange(1)

    wait(cz.at[pl.ds(0, LAST)], c_r.at[0])
    part = cz[0]
    for p in range(1, 8):
        part = part + cz[p]
    cm[0] = part
    send(cm.at[0], cm.at[1], c_s.at[1], c_r.at[1], (mate, v, g))

    wait(cm.at[1], c_r.at[1])
    sizes = jnp.sum(cm[0] + cm[1], axis=1, keepdims=True)
    own_size = jnp.sum(member * sizes, axis=0, keepdims=True)
    weight = masked * (NT * ROWS // SEGS) / own_size
    acc[...] = jnp.zeros_like(acc)

    wait(sb.at[pl.ds(1, 15)], t_r.at[1])

    def lse(first):
        top = sb[first, 0:1, :]
        for r in range(first + 1, first + 8):
            top = jnp.maximum(top, sb[r, 0:1, :])
        mass = jnp.zeros_like(top)
        for r in range(first, first + 8):
            mass = mass + sb[r, 1:2, :] * jnp.exp(sb[r, 0:1, :] - top)
        return top + jnp.log(mass)

    own_lse, other_lse = lse(0), lse(8)
    sc[...] = jnp.zeros_like(sc)
    sc[0:8, :] = jnp.where(sub == 0, own_lse, jnp.where(sub == 1, other_lse, weight))
    col[...] = sc[...].T

    sign = jnp.where(g == 0, -1.0, 1.0).astype(F32)

    def block(t, p):
        i = rem(div(z, 2) + 8 - off(p), 8)
        first = rem(2 * i + c * (15 + 2 * par), 16)
        rows = pl.ds(pl.multiple_of(TH * t, TH), TH)
        stats = col[rows, :]
        own_l, other_l, wgt = stats[:, 0:1], stats[:, 1:2], stats[:, 2:3]
        scale = (SOFTEN * sign) * wgt
        for n, k in enumerate((first, rem(first + 1, 16))):
            cols = pl.ds(pl.multiple_of(BLK * k, BLK), BLK)
            own_at = pl.ds(pl.multiple_of(COLS * g + BLK * k, BLK), BLK)
            log_own = lg[rows, own_at].astype(F32) * (1.0 / SOFTEN) - own_l
            log_other = ao[rows, cols].astype(F32) * (1.0 / SOFTEN) - other_l
            p_own = jnp.exp(log_own)
            p_other = jnp.exp(log_other)
            grad = (scale * (p_own - p_other)).astype(BF16)
            term = jnp.where(g == 0, p_own, p_other) * (log_own - log_other)
            acc[...] += wgt * (term[:, :128] + term[:, 128:])
            gn[rows, cols] = grad
            gb[p, rows, BLK * n:BLK * n + BLK] = grad

    def chunk(t):
        wait(ao.at[pl.ds(pl.multiple_of(TH * t, TH), TH)], x_r.at[t])
        pl.when(t < 2)(lambda: exchange(t + 2))
        there = pl.ds(pl.multiple_of(16 * t, 16), 16)

        def place(p):
            block(t, p)
            pl.when(t < 3)(lambda: ship_block(t, p))

        loop(0, LAST, place)
        block(t, LAST)
        mine = pl.ds(pl.multiple_of(TH * t + 16 * c, 16), 16)
        theirs = pl.ds(pl.multiple_of(TH * t + 16 * oc, 16), 16)
        grx[c, LAST, there, :] = gb[LAST, mine, :]
        send(gb.at[LAST, theirs], grx.at[c, LAST, there], g_s.at[4 + t], g_r.at[4 + t], core_mate)

    def ship_block(t, p):
        there = pl.ds(pl.multiple_of(16 * t, 16), 16)
        for e in range(2):
            here = pl.ds(pl.multiple_of(TH * t + 16 * e, 16), 16)
            send(
                gb.at[p, here], grx.at[c, p, there], g_s.at[t], g_r.at[t], (column(p), 2 * j + e, g)
            )

    loop(0, 4, chunk)

    out_own = pltpu.make_async_copy(gn, grad_out, s_loc.at[4])
    out_own.start()

    lp[0] = (acc[0:8] + acc[8:16] + acc[16:24] + acc[24:32]) * (-sign)
    loop(1, 16, lambda r: send(lp.at[0], lp.at[r], l_s.at[2], l_r.at[2], plane_dev(r, c)))

    wait(hb.at[c, 1 - my_pos], h_r.at[0])
    send(hb.at[c, 1 - my_pos], hb.at[c, 1 - my_pos], h_s.at[2], h_r.at[2], core_mate)

    out_row = lax.broadcasted_iota(jnp.int32, (128, 128), 0)
    in_row = lax.broadcasted_iota(jnp.int32, (128, 128), 1)
    source = ((out_row // 2) % 8) * 16 + (out_row // 16) * 2 + out_row % 2
    order = (in_row == source).astype(F32).astype(BF16)

    wait(hb.at[oc, rem(z + oc, 2)], h_r.at[1])
    wait(hb.at[oc, 1 - rem(z + oc, 2)], h_r.at[2])

    def loss_plane():
        wait(lp.at[pl.ds(1, 15)], l_r.at[2])
        part = lp[0]
        for r in range(1, 16):
            part = part + lp[r]
        lc[0] = part
        send(lc.at[0], lc.at[1], l_s.at[3], l_r.at[3], core_mate)

    def reduce(q):
        wait(rb.at[q, pl.ds(1, 15)], p_r.at[q])
        total = pb[q, g, j].astype(F32)
        for r in range(1, 16):
            total = total + rb[q, r].astype(F32)
        rsum[q] = total

    def multiply(q):
        rows = pl.ds(pl.multiple_of(16 * q, 16), 16)

        @pl.when(q == 3)
        def _():
            reduce(2)
            for done in range(3):
                pack(done)

        @pl.when(q == 0)
        def _():
            wait(grx.at[:, pl.ds(0, LAST), rows], g_s.at[q])
            loop(0, LAST, lambda p: ship_block(q + 3, p))

        wait(grx.at[:, pl.ds(0, LAST), rows], g_r.at[q])
        wait(grx.at[oc, LAST, rows], g_r.at[4 + q])
        xs = []
        for b in range(2):
            x = grx[b, :, rows, :].reshape(128, 2 * BLK)
            xs.append(jnp.dot(order, x, preferred_element_type=F32).astype(BF16))
        def share(r):
            j2, g2 = plane(r)
            send(pb.at[q, g2, j2], rb.at[q, r], p_s.at[q], p_r.at[q], (z, j2 * 2 + c, g2))

        for gg, first, last in ((og, 8, 16), (g, 1, 8)):
            cols = pl.ds(pl.multiple_of(HH * gg, 128), HH)
            part = jnp.dot(
                xs[0], hb[0, :, :, cols].reshape(512, HH), preferred_element_type=F32
            ) + jnp.dot(xs[1], hb[1, :, :, cols].reshape(512, HH), preferred_element_type=F32)
            pb[q, gg] = part.astype(BF16).reshape(8, 16, HH)
            loop(first, last, share)

        @pl.when((q == 1) | (q == 2))
        def _():
            reduce(q - 1)

        pl.when(q == 1)(loss_plane)
        pl.when(q == 3)(lambda: spread(0, 3, 0))

    def pack(q):
        for p in range(8):
            pair = rsum[q, 2 * p:2 * p + 2]
            x = jnp.concatenate(
                [pair[:, 128 * k:128 * k + 128] for k in range(7)] + [jnp.zeros((2, 128), F32)], axis=0
            )
            if p == LAST:
                own[:, 128 * q:128 * q + 128] = x
            else:
                zs[p, :, 128 * q:128 * q + 128] = x.astype(BF16)

    def spread(first, last, k):
        cols = slice(128 * first, 128 * last)
        for p in range(LAST):
            send(
                zs.at[p, :, cols], zr.at[p, :, cols], z_s.at[k], z_r.at[k],
                (rem(z + 2 * off(p), NT), v, g),
            )

    loop(0, 4, multiply)
    wait(lc.at[1], l_r.at[3])
    lz[LAST] = lc[0] + lc[1]
    loop(0, LAST, lambda p: send(lz.at[LAST], lz.at[p], l_s.at[0], l_r.at[0], (column(p), v, g)))
    reduce(3)
    pack(3)
    spread(3, 4, 1)

    slot = 8 * c + j

    def gather(first, last, k):
        cols = slice(128 * first, 128 * last)
        wait(zr.at[:, :, cols], z_r.at[k])
        total = own[:, cols]
        for p in range(LAST):
            total = total + zr[p, :, cols].astype(F32)
        fb[slot, :, cols] = total
        mine = fb.at[slot, :, cols]
        loop(1, 8, lambda r: send(mine, mine, f_s.at[k], f_r.at[k], plane_dev(r, c)))
        loop(0, 8, lambda r: send(mine, mine, f_s.at[k], f_r.at[k], plane_dev(r, oc)))

    gather(0, 3, 0)
    gather(3, 4, 1)

    wait(lz.at[pl.ds(0, LAST)], l_r.at[0])
    part = lz[0]
    for p in range(1, 8):
        part = part + lz[p]
    lm[0] = part
    send(lm.at[0], lm.at[1], l_s.at[1], l_r.at[1], (mate, v, g))

    loop(0, 4, lambda t: wait(ao.at[pl.ds(0, TH)], x_s.at[t]))
    for t in range(4):
        rows = pl.ds(16 * t, 16)
        if t >= 1:
            wait(grx.at[:, pl.ds(0, LAST), rows], g_s.at[t])
        wait(grx.at[0, LAST, rows], g_s.at[4 + t])
    loop(0, 3, lambda k: wait(hb.at[0, 0], h_s.at[k]))
    wait(cz.at[pl.ds(0, LAST)], c_s.at[0])
    wait(cm.at[1], c_s.at[1])
    wait(st.at[1], t_s.at[0])
    wait(sb.at[pl.ds(1, 15)], t_s.at[1])
    out_own.wait()
    loop(0, 4, lambda q: wait(rb.at[q, pl.ds(1, 15)], p_s.at[q]))
    wait(zr.at[:, :, 0:384], z_s.at[0])
    wait(zr.at[:, :, 384:512], z_s.at[1])
    wait(lz.at[pl.ds(0, LAST)], l_s.at[0])
    wait(lm.at[1], l_s.at[1])
    wait(lp.at[pl.ds(1, 15)], l_s.at[2])
    wait(lc.at[1], l_s.at[3])
    wait(lm.at[1], l_r.at[1])
    loss_out[...] = jnp.sum(lm[0] + lm[1], keepdims=True) * (SOFTEN * SOFTEN) / (NT * ROWS)

    def assemble(t):
        for e in range(2):
            for h in range(2):
                n = 8 * e + 4 * h
                row = TH * t + 16 * e + 8 * h
                for k in range(7):
                    hid_out[row:row + 8, 128 * k:128 * k + 128] = jnp.concatenate(
                        [fb[n + i, 2 * k:2 * k + 2, 128 * t:128 * t + 128] for i in range(4)], axis=0
                    )

    wait(fb.at[pl.ds(0, 15), :, 0:384], f_r.at[0])
    for t in range(3):
        assemble(t)
    wait(fb.at[pl.ds(0, 15), :, 0:384], f_s.at[0])
    wait(fb.at[pl.ds(0, 15), :, 384:512], f_r.at[1])
    assemble(3)
    wait(fb.at[pl.ds(0, 15), :, 384:512], f_s.at[1])


def per_device(logits, segment_ids, token_mask, student_head):
    dma = pltpu.SemaphoreType.DMA
    any_space = pl.BlockSpec(memory_space=pl.ANY)
    vmem_space = pl.BlockSpec(memory_space=pltpu.VMEM)
    grad, hidden, loss = pl.pallas_call(
        kernel,
        out_shape=(
            jax.ShapeDtypeStruct((ROWS, COLS), BF16),
            jax.ShapeDtypeStruct((ROWS, HH), F32),
            jax.ShapeDtypeStruct((1, 1), F32),
        ),
        in_specs=[any_space] * 4,
        out_specs=(any_space, vmem_space, vmem_space),
        scratch_shapes=[
            pltpu.VMEM((ROWS, 2 * COLS), BF16),
            pltpu.VMEM((ROWS, COLS), BF16),
            pltpu.VMEM((8, ROWS, 2 * BLK), BF16),
            pltpu.VMEM((ROWS, COLS), BF16),
            pltpu.VMEM((2, 8, HALF, 2 * BLK), BF16),
            pltpu.VMEM((2, 2, BLK, HS), BF16),
            pltpu.VMEM((4, 2, 8, 16, HH), BF16),
            pltpu.VMEM((4, 16, 16, HH), BF16),
            pltpu.VMEM((4, 16, HH), F32),
            pltpu.VMEM((LAST, 16, 512), BF16),
            pltpu.VMEM((LAST, 16, 512), BF16),
            pltpu.VMEM((16, 512), F32),
            pltpu.VMEM((16, 16, 512), F32),
            pltpu.VMEM((128, 128), F32),
            pltpu.VMEM((128, 128), F32),
            pltpu.VMEM((2, 8, 128), F32),
            pltpu.VMEM((16, 8, 128), F32),
            pltpu.VMEM((8, 8, 128), F32),
            pltpu.VMEM((2, 8, 128), F32),
            pltpu.VMEM((TH, 128), F32),
            pltpu.VMEM((8, 8, 128), F32),
            pltpu.VMEM((2, 8, 128), F32),
            pltpu.VMEM((16, 8, 128), F32),
            pltpu.VMEM((2, 8, 128), F32),
            pltpu.VMEM((1, ROWS), jnp.int32),
            pltpu.VMEM((1, ROWS), jnp.int32),
            dma((5,)),
            dma((4,)), dma((4,)),
            dma((3,)), dma((3,)),
            dma((2,)), dma((2,)),
            dma((2,)), dma((2,)),
            dma((8,)), dma((8,)),
            dma((4,)), dma((4,)),
            dma((2,)), dma((2,)),
            dma((2,)), dma((2,)),
            dma((4,)), dma((4,)),
        ],
        compiler_params=pltpu.CompilerParams(
            collective_id=0, has_side_effects=True, vmem_limit_bytes=VMEM_BYTES
        ),
        cost_estimate=pl.CostEstimate(
            flops=2 * ROWS * COLS * HS, bytes_accessed=6 * 1024 * 1024, transcendentals=3 * ROWS * COLS
        ),
        name="distill",
    )(
        logits.reshape(ROWS, 2 * COLS),
        segment_ids.reshape(1, ROWS),
        token_mask.reshape(1, ROWS),
        student_head.reshape(BLK, HS),
    )
    return grad, hidden, loss.reshape(())


def solution(mesh):
    placed = (P("grp", "tok", "vocab"), P("tok"), P("tok"), P(("vocab", "grp"), "tok", None, None))
    return jax.shard_map(
        per_device,
        mesh=mesh,
        in_specs=placed,
        out_specs=(P("tok", ("vocab", "grp")), P("tok", "grp"), P()),
        check_vma=False,
    )
```
